128 devices in a mesh: space: 32 (over x, z_hi, y), orb: 4 (over z_lo, core).
Axes of the slice: x: 4, y: 4, z: 4 (z_hi: 2, z_lo: 2; z = z_hi * 2 + z_lo), core: 2. Of those that a mesh axis runs over, the one named last changes fastest.
Arguments:
- orbitals: float32 [256, 16, 32, 512], P('space', None, None, 'orb'), may hold values from -75 to 75
- potential: float32 [256, 16, 32], P('space'), may hold values from -2 to 0
Outputs:
- whitened: float32 [256, 16, 32, 512], P('space', None, None, 'orb')
The draws below stay inside these ranges and needn't reach their ends.
All inputs are finite; a program needn't handle non-finite values.
Results may differ from the reference program's by a relative error of at most 0.0003.
Values sent between devices are 32-bit elements; how exact they have to be, the bound alone decides.
No kernel may reach another device: no remote copies, remote signals or barrier semaphores. Data moves between devices by JAX's collectives and lax.ppermute only.
A program may use at most 192 MiB of HBM per device.

```python
import math
import jax
import jax.numpy as jnp
from jax import lax

NY = 16
NZ = 32
NORB = 512
DEGREE = 4
NS_ITERS = 8
NX = 256
NCELLS = 131072


def draw_orbitals(key, part):
    key = jax.random.fold_in(key, 11)
    base_key, scale_key = jax.random.split(key, 2)
    base_values = jnp.clip(jax.random.normal(base_key, (NX, NY, NZ, NORB), jnp.float32), -5.0, 5.0)
    mixed = base_values + 0.4 * jnp.roll(base_values, 1, axis=3)
    column_scales = jnp.exp(jax.random.uniform(scale_key, (NORB,), jnp.float32, 0.0, math.log(10.0)))
    return (mixed * column_scales).astype(jnp.float32)


def block_levels(rng, extent, cuts, least, top_value):
    loudness, own = 1.0, jax.random.fold_in(rng, 6)
    for axis_at, parts in cuts:
        heights = jnp.exp(jax.random.uniform(jax.random.fold_in(own, axis_at), (parts,), jnp.float32, least / len(cuts), top_value / len(cuts)))
        loudness = loudness * jnp.repeat(heights, extent[axis_at] // parts).reshape([-1 if axis == axis_at else 1 for axis in range(len(extent))])
    return loudness


def setup_inputs(seed: int = 0) -> dict:
    splits = jax.random.split(jax.random.key(seed), 3)
    return {
        "orbitals": draw_orbitals(jax.random.fold_in(splits[2], 71), 0),
        "potential": jnp.clip(-2.0 + 2.0 * jax.random.uniform(splits[1], (NX, NY, NZ), jnp.float32) ** block_levels(splits[1], (NX, NY, NZ), ((0, 32),), -0.2, 0.2), -2.0, 0.0),
    }


STENCIL_WEIGHTS = [-49.0 / 18.0, 3.0 / 2.0, -3.0 / 20.0, 1.0 / 90.0]
CENTER = 5.0
HALF_WIDTH = 4.0

def apply_hamiltonian(field, potential):
    laplace = 3.0 * STENCIL_WEIGHTS[0] * field
    for offset in range(1, 4):
        for axis_number in range(3):
            laplace = laplace + STENCIL_WEIGHTS[offset] * (jnp.roll(field, offset, axis_number) + jnp.roll(field, -offset, axis_number))
    return -0.5 * laplace + potential[..., None] * field

def whiten_factor(intersection):
    norm_scale = jnp.sqrt(jnp.sum(intersection * intersection) + 1e-06)
    identity = jnp.eye(intersection.shape[0], dtype=jnp.float32)
    scaled = intersection / norm_scale
    inverse = identity
    for step in range(NS_ITERS):
        factor = 1.5 * identity - 0.5 * jnp.dot(inverse, scaled, precision=lax.Precision.HIGHEST)
        scaled = jnp.dot(scaled, factor, precision=lax.Precision.HIGHEST)
        inverse = jnp.dot(factor, inverse, precision=lax.Precision.HIGHEST)
    return inverse / jnp.sqrt(norm_scale)

def reference(orbitals, potential):
    previous = orbitals
    current = (apply_hamiltonian(orbitals, potential) - CENTER * orbitals) / HALF_WIDTH
    for degree_step in range(2, DEGREE + 1):
        following = 2.0 * (apply_hamiltonian(current, potential) - CENTER * current) / HALF_WIDTH - previous
        previous = current
        current = following
    cell_rows = current.reshape(-1, current.shape[-1])
    intersection = jnp.dot(cell_rows.T, cell_rows, precision=lax.Precision.HIGHEST) / NCELLS
    root_inverse = whiten_factor(intersection)
    whitened = jnp.dot(cell_rows, root_inverse, precision=lax.Precision.HIGHEST)
    return whitened.reshape(current.shape)
```

```python
import numpy as np
import jax
import jax.numpy as jnp
from jax import lax
from jax.experimental import pallas as pl
from jax.experimental.pallas import tpu as pltpu
from jax.sharding import Mesh, PartitionSpec as P

DEGREE = 4
NS_ITERS = 8
NY, NZ = 16, 32
PLANE = NY * NZ
NX = 256
NORB = 512
SLAB = 8
SPACE = ("x", "zh", "y")
ORB = ("zl", "c")
EVERY = SPACE + ORB
F32 = jnp.float32
BF16 = jnp.bfloat16
VMEM = 56 * 1024 * 1024

STENCIL = (270.0, -27.0, 2.0)
UNIT = -0.5 / 180.0 / 4.0
DIAGONAL = (1.5 * 49.0 / 18.0 - 5.0) / 4.0


def plane_stencil():
    def ring(n):
        m = np.zeros((n, n), np.float32)
        for k, w in enumerate(STENCIL, 1):
            for i in range(n):
                m[i, (i + k) % n] += w
                m[i, (i - k) % n] += w
        return m

    return np.kron(ring(NY), np.eye(NZ, dtype=np.float32)) + np.kron(
        np.eye(NY, dtype=np.float32), ring(NZ)
    )


def low_rows(shape):
    return lax.broadcasted_iota(jnp.int32, shape, len(shape) - 2) < 4


def swap_halves(a):
    return pltpu.roll(a, 4, a.ndim - 2)


def split(a):
    hi = a.astype(BF16)
    return hi, (a - hi.astype(F32)).astype(BF16)


def dot(a, b):
    return jnp.dot(a, b, preferred_element_type=F32)


def dot3(a, b):
    return dot(a[0], b[0]) + (dot(a[0], b[1]) + dot(a[1], b[0]))


def spread_kernel(v_ref, pot_ref, out_ref):
    step = pl.program_id(0)

    @pl.when(step < 4)
    def _():
        a = v_ref[0].T.reshape(16, 8, PLANE)
        b = v_ref[1].T.reshape(16, 8, PLANE)
        low = low_rows(a.shape)
        out_ref[:, 0] = jnp.where(low, a, swap_halves(b))
        out_ref[:, 1] = jnp.where(low, swap_halves(a), b)

    @pl.when(step == 4)
    def _():
        out_ref[...] = jnp.broadcast_to(pot_ref[...], out_ref.shape)


def spread(field, potential):
    out = pl.pallas_call(
        spread_kernel,
        grid=(5,),
        in_specs=[
            pl.BlockSpec((2, PLANE, 128), lambda i: (jnp.minimum(i, 3), 0, 0)),
            pl.BlockSpec((SLAB, PLANE), lambda i: (0, 0)),
        ],
        out_specs=pl.BlockSpec((16, 2, 8, PLANE), lambda i: (0, 0, i, 0)),
        out_shape=jax.ShapeDtypeStruct((16, 2, 40, PLANE), F32),
        compiler_params=pltpu.CompilerParams(vmem_limit_bytes=VMEM),
        name="spread",
    )(field, potential)
    return out.reshape(32 * 40, PLANE)


ROWS = 4 * NX
EDGE = 16
CHUNK = 256


def filter_kernel(in_ref, ring_ref, out_ref, one_ref, two_ref, diag_ref):
    def fill(s, _):
        base = pl.multiple_of(s * 32, 32)
        one_ref[pl.ds(EDGE + base, 32), :] = in_ref[s, 0:32, :]
        pot = in_ref[s, 32:40, :]
        low = low_rows((8, PLANE))
        for t in range(4):
            row = jnp.where(low, pot[2 * t : 2 * t + 1], pot[2 * t + 1 : 2 * t + 2])
            diag_ref[pl.ds(base + 8 * t, 8), :] = 0.25 * row + DIAGONAL
        return 0

    lax.fori_loop(0, 32, fill, 0)
    ring = ring_ref[...]

    def close(ref):
        ref[0:EDGE, :] = ref[ROWS : ROWS + EDGE, :]
        ref[ROWS + EDGE :, :] = ref[EDGE : 2 * EDGE, :]

    def apply(cur_ref, base):
        wide = cur_ref[pl.ds(base, CHUNK + 2 * EDGE), :]
        cur = wide[EDGE : EDGE + CHUNK]
        hi, lo = split(cur)
        both = dot(jnp.concatenate([hi, lo], axis=0), ring)
        near = both[:CHUNK] + both[CHUNK:]
        half = pltpu.roll(wide, 4, 0)

        def at(a, shift):
            return a[EDGE + shift : EDGE + shift + CHUNK]

        along = (
            STENCIL[0] * (at(half, 0) + at(half, 8))
            + STENCIL[1] * (at(wide, 8) + at(wide, -8))
            + STENCIL[2] * (at(half, -8) + at(half, 16))
        )
        return UNIT * (near + along) + diag_ref[pl.ds(base, CHUNK), :] * cur, cur

    def sweep(body):
        def run(i, _):
            body(pl.multiple_of(i * CHUNK, CHUNK))
            return 0

        lax.fori_loop(0, ROWS // CHUNK, run, 0)

    close(one_ref)

    def first(base):
        value, _ = apply(one_ref, base)
        two_ref[pl.ds(EDGE + base, CHUNK), :] = value

    sweep(first)
    previous, current = one_ref, two_ref
    for degree_step in range(2, DEGREE + 1):
        close(current)
        last = degree_step == DEGREE

        def following(base, previous=previous, current=current, last=last):
            value, _ = apply(current, base)
            value = 2.0 * value - previous[pl.ds(EDGE + base, CHUNK), :]
            if last:
                out_ref[pl.ds(base, CHUNK), :] = value
            else:
                previous[pl.ds(EDGE + base, CHUNK), :] = value

        sweep(following)
        previous, current = current, previous


def chebyshev(spread_cells, ring):
    return pl.pallas_call(
        filter_kernel,
        out_shape=jax.ShapeDtypeStruct((ROWS, PLANE), F32),
        scratch_shapes=[
            pltpu.VMEM((ROWS + 2 * EDGE, PLANE), F32),
            pltpu.VMEM((ROWS + 2 * EDGE, PLANE), F32),
            pltpu.VMEM((ROWS, PLANE), F32),
        ],
        compiler_params=pltpu.CompilerParams(vmem_limit_bytes=VMEM),
        name="chebyshev",
    )(spread_cells.reshape(32, 40, PLANE), ring)


def gram_kernel(in_ref, hi_ref, lo_ref, gram_ref, cells_ref):
    for q in range(4):
        a = in_ref[:, 0, q]
        b = in_ref[:, 1, q]
        low = low_rows(a.shape)
        rows = pl.ds(128 * q, 128)
        cells_ref[rows, :PLANE] = jnp.where(low, a, swap_halves(b)).reshape(128, PLANE)
        cells_ref[rows, PLANE:] = jnp.where(low, swap_halves(a), b).reshape(128, PLANE)
    by_orbital = cells_ref[...]
    left = split(by_orbital)
    right = split(by_orbital.T)
    hi_ref[...] = right[0]
    lo_ref[...] = right[1]
    gram = dot3(left, right)
    for k in range(4):
        gram_ref[k] = gram[:, 128 * k : 128 * (k + 1)]


def gram(cells):
    return pl.pallas_call(
        gram_kernel,
        out_shape=(
            jax.ShapeDtypeStruct((2 * PLANE, NORB), BF16),
            jax.ShapeDtypeStruct((2 * PLANE, NORB), BF16),
            jax.ShapeDtypeStruct((4, NORB, 128), F32),
        ),
        scratch_shapes=[pltpu.VMEM((NORB, 2 * PLANE), F32)],
        compiler_params=pltpu.CompilerParams(vmem_limit_bytes=VMEM),
        name="gram",
    )(cells.reshape(16, 2, 4, 8, PLANE))


def whiten_kernel(gram_ref, hi_ref, lo_ref, out_ref):
    total = jnp.concatenate([gram_ref[k] for k in range(4)], axis=1)
    total = total * (1.0 / (NX * PLANE))
    square = jnp.sum(jnp.sum(total * total, axis=0, keepdims=True), axis=1, keepdims=True)
    norm_scale = jnp.sqrt(square + 1e-06)
    row = lax.broadcasted_iota(jnp.int32, (NORB, NORB), 0)
    col = lax.broadcasted_iota(jnp.int32, (NORB, NORB), 1)
    three_halves = jnp.where(row == col, 1.5, 0.0).astype(F32)
    scaled = total / norm_scale
    inverse = None
    for step in range(NS_ITERS):
        factor = three_halves - 0.5 * scaled
        parts = split(factor)
        inverse = factor if inverse is None else dot3(parts, split(inverse))
        if step < NS_ITERS - 1:
            scaled = dot3(split(dot3(split(scaled), parts)), parts)
    root = split(inverse / jnp.sqrt(norm_scale))
    white = dot3((hi_ref[...], lo_ref[...]), root)
    for k in range(4):
        out_ref[k] = white[:, 128 * k : 128 * (k + 1)]


def whiten(total, hi, lo):
    return pl.pallas_call(
        whiten_kernel,
        out_shape=jax.ShapeDtypeStruct((4, 2 * PLANE, 128), F32),
        compiler_params=pltpu.CompilerParams(vmem_limit_bytes=VMEM),
        name="whiten",
    )(total, hi, lo)


def exchange(a, axes):
    return lax.all_to_all(a, axes, 0, 0, tiled=True)


def body(orbitals, potential):
    ring = jnp.asarray(plane_stencil(), BF16)
    sent = spread(orbitals.reshape(SLAB, PLANE, 128), potential.reshape(SLAB, PLANE))
    filtered = chebyshev(exchange(sent, SPACE), ring)
    hi, lo, partial_terms = gram(exchange(filtered, EVERY))
    terms = exchange(partial_terms.reshape(4 * NORB, 128), EVERY)
    own = jnp.sum(terms.reshape(128, -1, 128), axis=0)
    total = exchange(jnp.tile(own, (128, 1)), EVERY).reshape(4, NORB, 128)
    whitened = exchange(whiten(total, hi, lo).reshape(8 * PLANE, 128), ORB)
    return whitened.reshape(orbitals.shape)


def solution(mesh):
    fine = Mesh(mesh.devices.reshape(4, 2, 4, 2, 2), EVERY)
    return jax.shard_map(
        body,
        mesh=fine,
        in_specs=(P(SPACE, None, None, ORB), P(SPACE, None, None)),
        out_specs=P(SPACE, None, None, ORB),
        check_vma=False,
    )
```

```python
import numpy as np
import jax
import jax.numpy as jnp
from jax import lax
from jax.experimental import pallas as pl
from jax.experimental.pallas import tpu as pltpu
from jax.sharding import Mesh, PartitionSpec as P

DEGREE = 4
NS_ITERS = 8
NY, NZ = 16, 32
PLANE = NY * NZ
NX = 256
NORB = 512
SLAB = 8
SPACE = ("x", "zh", "y")
ORB = ("zl", "c")
EVERY = SPACE + ORB
F32 = jnp.float32
BF16 = jnp.bfloat16
VMEM = 30 * 1024 * 1024
VMEM_SMALL = 24 * 1024 * 1024

STENCIL = (135.0, -13.5, 1.0)
UNIT = -0.5 / 90.0 / 4.0
DIAGONAL = (1.5 * 49.0 / 18.0 - 5.0) / 4.0


def plane_stencil():
    def ring(n):
        m = np.zeros((n, n), np.float32)
        for k, w in enumerate(STENCIL, 1):
            for i in range(n):
                m[i, (i + k) % n] += w
                m[i, (i - k) % n] += w
        return m

    return np.kron(ring(NY), np.eye(NZ, dtype=np.float32)) + np.kron(
        np.eye(NY, dtype=np.float32), ring(NZ)
    )


def low_rows(shape):
    return lax.broadcasted_iota(jnp.int32, shape, len(shape) - 2) < 4


def swap_halves(a):
    return pltpu.roll(a, 4, a.ndim - 2)


def split(a):
    hi = a.astype(BF16)
    return hi, (a - hi.astype(F32)).astype(BF16)


def dot(a, b):
    return jnp.dot(a, b, preferred_element_type=F32)


def dot3(a, b):
    return dot(a[0], b[0]) + (dot(a[0], b[1]) + dot(a[1], b[0]))


def spread_kernel(v_ref, pot_ref, out_ref):
    step = pl.program_id(0)

    @pl.when(step < 4)
    def _():
        a = v_ref[0].T.reshape(16, 8, PLANE)
        b = v_ref[1].T.reshape(16, 8, PLANE)
        low = low_rows(a.shape)
        out_ref[:, 0] = jnp.where(low, a, swap_halves(b))
        out_ref[:, 1] = jnp.where(low, swap_halves(a), b)

    @pl.when(step == 4)
    def _():
        out_ref[...] = jnp.broadcast_to(pot_ref[...], out_ref.shape)


def spread(field, potential):
    out = pl.pallas_call(
        spread_kernel,
        grid=(5,),
        in_specs=[
            pl.BlockSpec((2, PLANE, 128), lambda i: (jnp.minimum(i, 3), 0, 0)),
            pl.BlockSpec((SLAB, PLANE), lambda i: (0, 0)),
        ],
        out_specs=pl.BlockSpec((16, 2, 8, PLANE), lambda i: (0, 0, i, 0)),
        out_shape=jax.ShapeDtypeStruct((16, 2, 40, PLANE), F32),
        compiler_params=pltpu.CompilerParams(vmem_limit_bytes=VMEM),
        name="spread",
    )(field, potential)
    return out.reshape(32 * 40, PLANE)


ROWS = 4 * NX
EDGE = 16
CHUNK = 256
UNROLL = False


def filter_kernel(in_ref, ring_ref, out_ref, one_ref, two_ref, diag_ref):
    def fill(s, _):
        base = pl.multiple_of(s * 32, 32)
        one_ref[pl.ds(EDGE + base, 32), :] = in_ref[s, 0:32, :]
        pot = in_ref[s, 32:40, :]
        low = low_rows((8, PLANE))
        for t in range(4):
            row = jnp.where(low, pot[2 * t : 2 * t + 1], pot[2 * t + 1 : 2 * t + 2])
            diag_ref[pl.ds(base + 8 * t, 8), :] = 0.5 * row + 2.0 * DIAGONAL
        return 0

    lax.fori_loop(0, 32, fill, 0)
    ring = ring_ref[...]

    def close(ref):
        ref[0:EDGE, :] = ref[ROWS : ROWS + EDGE, :]
        ref[ROWS + EDGE :, :] = ref[EDGE : 2 * EDGE, :]

    def twice(cur_ref, base):
        wide = cur_ref[pl.ds(base, CHUNK + 2 * EDGE), :]
        cur = wide[EDGE : EDGE + CHUNK]
        near = dot(jnp.concatenate(split(cur), axis=1), ring)
        half = pltpu.roll(wide, 4, 0)

        def at(a, shift):
            return a[EDGE + shift : EDGE + shift + CHUNK]

        along = (
            STENCIL[0] * (at(half, 0) + at(half, 8))
            + STENCIL[1] * (at(wide, 8) + at(wide, -8))
            + (at(half, -8) + at(half, 16))
        )
        return (2.0 * UNIT) * (near + along) + diag_ref[pl.ds(base, CHUNK), :] * cur

    def sweep(body):
        if UNROLL:
            for i in range(ROWS // CHUNK):
                body(i * CHUNK)
            return

        def run(i, _):
            body(pl.multiple_of(i * CHUNK, CHUNK))
            return 0

        lax.fori_loop(0, ROWS // CHUNK, run, 0)

    close(one_ref)

    def first(base):
        two_ref[pl.ds(EDGE + base, CHUNK), :] = 0.5 * twice(one_ref, base)

    sweep(first)
    previous, current = one_ref, two_ref
    for degree_step in range(2, DEGREE + 1):
        close(current)
        last = degree_step == DEGREE

        def following(base, previous=previous, current=current, last=last):
            value = twice(current, base) - previous[pl.ds(EDGE + base, CHUNK), :]
            if last:
                out_ref[pl.ds(base, CHUNK), :] = value
            else:
                previous[pl.ds(EDGE + base, CHUNK), :] = value

        sweep(following)
        previous, current = current, previous


def chebyshev(spread_cells, ring):
    return pl.pallas_call(
        filter_kernel,
        out_shape=jax.ShapeDtypeStruct((ROWS, PLANE), F32),
        scratch_shapes=[
            pltpu.VMEM((ROWS + 2 * EDGE, PLANE), F32),
            pltpu.VMEM((ROWS + 2 * EDGE, PLANE), F32),
            pltpu.VMEM((ROWS, PLANE), F32),
        ],
        compiler_params=pltpu.CompilerParams(vmem_limit_bytes=VMEM),
        name="chebyshev",
    )(spread_cells.reshape(32, 40, PLANE), ring)


BLOCKS = tuple((i, j) for i in range(4) for j in range(i, 4))
PART = 384


def gram_kernel(in_ref, near_ref, far_ref, gram_ref, cells_ref):
    for q in range(4):
        a = in_ref[:, 0, q]
        b = in_ref[:, 1, q]
        low = low_rows(a.shape)
        rows = pl.ds(128 * q, 128)
        cells_ref[rows, :PLANE] = jnp.where(low, a, swap_halves(b)).reshape(128, PLANE)
        cells_ref[rows, PLANE:] = jnp.where(low, swap_halves(a), b).reshape(128, PLANE)
    by_orbital = cells_ref[...]
    by_cell = by_orbital.T
    near_ref[...] = by_cell[:PART]
    far_ref[...] = by_cell[PART:]
    left, right = split(by_orbital), split(by_cell)
    top = dot3([p[:256] for p in left], right)
    low_block = dot3([p[256:] for p in left], [p[:, 256:] for p in right])
    for k, (i, j) in enumerate(BLOCKS):
        part, i, j = (top, i, j) if i < 2 else (low_block, i - 2, j - 2)
        gram_ref[128 * k : 128 * (k + 1), :] = part[
            128 * i : 128 * (i + 1), 128 * j : 128 * (j + 1)
        ]


def gram(cells):
    return pl.pallas_call(
        gram_kernel,
        out_shape=(
            jax.ShapeDtypeStruct((PART, NORB), F32),
            jax.ShapeDtypeStruct((2 * PLANE - PART, NORB), F32),
            jax.ShapeDtypeStruct((128 * len(BLOCKS), 128), F32),
        ),
        scratch_shapes=[pltpu.VMEM((NORB, 2 * PLANE), F32)],
        compiler_params=pltpu.CompilerParams(vmem_limit_bytes=VMEM),
        name="gram",
    )(cells.reshape(16, 2, 4, 8, PLANE))


def product(a, b):
    top = dot3([p[:256] for p in a], b)
    low_block = dot3([p[256:] for p in a], [p[:, 256:] for p in b])
    return jnp.concatenate(
        [top, jnp.concatenate([top[:, 256:].T, low_block], axis=1)], axis=0
    )


def root_kernel(gram_ref, out_ref):
    blocks = {}
    for k, (i, j) in enumerate(BLOCKS):
        block = gram_ref[128 * k : 128 * (k + 1), :] * (1.0 / (NX * PLANE))
        blocks[i, j] = block
        if i != j:
            blocks[j, i] = block.T
    total = jnp.concatenate(
        [jnp.concatenate([blocks[i, j] for j in range(4)], axis=1) for i in range(4)], axis=0
    )
    square = jnp.sum(jnp.sum(total * total, axis=0, keepdims=True), axis=1, keepdims=True)
    norm_scale = jnp.sqrt(square + 1e-06)
    row = lax.broadcasted_iota(jnp.int32, (NORB, NORB), 0)
    col = lax.broadcasted_iota(jnp.int32, (NORB, NORB), 1)
    diagonal = row == col
    m = total / norm_scale
    inverse = None
    for pair in range(NS_ITERS // 2):
        parts = split(m)
        m2 = product(parts, parts)
        tail = product(split(m2), split(0.0625 * m2 - 0.5625 * m))
        factor = (jnp.where(diagonal, 2.25, 0.0) - 2.4375 * m) + (1.6875 * m2 + tail)
        factors = split(factor)
        inverse = factor if inverse is None else product(split(inverse), factors)
        if pair < NS_ITERS // 2 - 1:
            m = product(parts, split(product(factors, factors)))
    root = split(inverse / jnp.sqrt(norm_scale))
    for h in range(2):
        for k in range(4):
            out_ref[h, k] = root[h][:, 128 * k : 128 * (k + 1)]


def inverse_root(total):
    return pl.pallas_call(
        root_kernel,
        out_shape=jax.ShapeDtypeStruct((2, 4, NORB, 128), BF16),
        compiler_params=pltpu.CompilerParams(vmem_limit_bytes=VMEM),
        name="inverse_root",
    )(total)


def whiten_kernel(place_ref, *refs):
    chunks, root_ref, out_ref = refs[:4], refs[4], refs[5]
    root = (root_ref[0, 0], root_ref[1, 0])
    for part in range(2):

        @pl.when(pl.program_id(0) == part)
        def _():
            near, far = chunks[2 * part : 2 * part + 2]
            out_ref[0, 0, :PART] = dot3(split(near[...]), root)
            out_ref[0, 0, PART:] = dot3(split(far[...]), root)


def whiten(place, chunks, root, whole):
    def slot(i, p):
        return (jnp.where(i == 0, p[0], 1 - p[0]), p[2] if whole else 0, 0, 0)

    def all_of(a):
        return pl.BlockSpec(a.shape, lambda i, p: (0, 0))

    return pl.pallas_call(
        whiten_kernel,
        grid_spec=pltpu.PrefetchScalarGridSpec(
            num_scalar_prefetch=1,
            grid=(2,),
            in_specs=[all_of(a) for a in chunks]
            + [pl.BlockSpec((2, 1, NORB, 128), lambda i, p: (0, p[1], 0, 0))],
            out_specs=pl.BlockSpec((1, 1, 2 * PLANE, 128), slot),
        ),
        out_shape=jax.ShapeDtypeStruct((2, 2 if whole else 1, 2 * PLANE, 128), F32),
        compiler_params=pltpu.CompilerParams(vmem_limit_bytes=VMEM_SMALL),
        name="whiten",
    )(place, *chunks, root)


def exchange(a, axes):
    return lax.all_to_all(a, axes, 0, 0, tiled=True)


def swap(a, axis):
    return lax.ppermute(a, axis, [(0, 1), (1, 0)])


def body(orbitals, potential):
    zl, c = lax.axis_index("zl"), lax.axis_index("c")
    ring = jnp.asarray(np.tile(plane_stencil(), (2, 1)), BF16)
    sent = spread(orbitals.reshape(SLAB, PLANE, 128), potential.reshape(SLAB, PLANE))
    filtered = chebyshev(exchange(sent, SPACE), ring)
    near, far, terms = gram(exchange(filtered, EVERY))

    other_near = swap(near, "zl")
    halves = terms.reshape(2, -1, 128)
    own = lax.dynamic_index_in_dim(halves, c, 0, False)
    own = own + swap(lax.dynamic_index_in_dim(halves, 1 - c, 0, False), "c")
    share = exchange(own, ("x", "y"))
    share = jnp.sum(share.reshape(16, -1, 128), axis=0)
    share, other_near = lax.optimization_barrier((share, other_near))
    share = share + swap(share, "zl")
    share = share + swap(share, "zh")
    share, far = lax.optimization_barrier((share, far))
    other_far = swap(far, "zl")
    own = exchange(jnp.tile(share, (16, 1)), ("x", "y"))
    sibling = swap(own, "c")
    total = jnp.where(
        c == 0, jnp.concatenate([own, sibling]), jnp.concatenate([sibling, own])
    )
    root = inverse_root(total)

    chunks = (near, far, other_near, other_far)
    theirs = whiten(jnp.stack([zl, 2 * zl + 1 - c, c]), chunks, root, False)
    ours = whiten(jnp.stack([zl, 2 * zl + c, c]), chunks, root, True)
    whitened = lax.dynamic_update_slice(ours, swap(theirs, "c"), (0, 1 - c, 0, 0))
    return whitened.reshape(orbitals.shape)


def solution(mesh):
    fine = Mesh(mesh.devices.reshape(4, 2, 4, 2, 2), EVERY)
    return jax.shard_map(
        body,
        mesh=fine,
        in_specs=(P(SPACE, None, None, ORB), P(SPACE, None, None)),
        out_specs=P(SPACE, None, None, ORB),
        check_vma=False,
    )
```

```python
import functools

import numpy as np
import jax
import jax.numpy as jnp
from jax import lax
from jax.experimental import pallas as pl
from jax.experimental.pallas import tpu as pltpu
from jax.sharding import Mesh, PartitionSpec as P

DEGREE = 4
NS_ITERS = 8
NY, NZ = 16, 32
PLANE = NY * NZ
NX = 256
NORB = 512
SLAB = 8
SPACE = ("x", "zh", "y")
ORB = ("zl", "c")
EVERY = SPACE + ORB
F32 = jnp.float32
BF16 = jnp.bfloat16
VMEM = 30 * 1024 * 1024
VMEM_SMALL = 24 * 1024 * 1024

STENCIL = (135.0, -13.5, 1.0)
UNIT = -0.5 / 90.0 / 4.0
DIAGONAL = (1.5 * 49.0 / 18.0 - 5.0) / 4.0


def plane_stencil():
    def ring(n):
        m = np.zeros((n, n), np.float32)
        for k, w in enumerate(STENCIL, 1):
            for i in range(n):
                m[i, (i + k) % n] += w
                m[i, (i - k) % n] += w
        return m

    return np.kron(ring(NY), np.eye(NZ, dtype=np.float32)) + np.kron(
        np.eye(NY, dtype=np.float32), ring(NZ)
    )


def low_rows(shape):
    return lax.broadcasted_iota(jnp.int32, shape, len(shape) - 2) < 4


def swap_halves(a):
    return pltpu.roll(a, 4, a.ndim - 2)


def split(a):
    hi = a.astype(BF16)
    return hi, (a - hi.astype(F32)).astype(BF16)


def dot(a, b):
    return jnp.dot(a, b, preferred_element_type=F32)


def dot_wide(a, b):
    wide = jnp.concatenate(b, axis=1)
    high, low = dot(a[0], wide), dot(a[1], wide)
    n = b[0].shape[1]
    return high[:, :n] + (high[:, n:] + low[:, :n])


def dot3(a, b):
    return dot(a[0], b[0]) + (dot(a[0], b[1]) + dot(a[1], b[0]))


def spread_kernel(v_ref, pot_ref, out_ref):
    step = pl.program_id(0)

    @pl.when(step < 4)
    def _():
        a = v_ref[0].T.reshape(16, 8, PLANE)
        b = v_ref[1].T.reshape(16, 8, PLANE)
        low = low_rows(a.shape)
        out_ref[:, 0] = jnp.where(low, a, swap_halves(b))
        out_ref[:, 1] = jnp.where(low, swap_halves(a), b)

    @pl.when(step == 4)
    def _():
        pot = jnp.concatenate([pot_ref[:, y, :] for y in range(NY)], axis=1)
        out_ref[...] = jnp.broadcast_to(pot, out_ref.shape)


def spread(field, potential):
    out = pl.pallas_call(
        spread_kernel,
        grid=(5,),
        in_specs=[
            pl.BlockSpec((2, PLANE, 128), lambda i: (jnp.minimum(i, 3), 0, 0)),
            pl.BlockSpec((SLAB, NY, NZ), lambda i: (0, 0, 0)),
        ],
        out_specs=pl.BlockSpec((16, 2, 8, PLANE), lambda i: (0, 0, i, 0)),
        out_shape=jax.ShapeDtypeStruct((16, 2, 40, PLANE), F32),
        compiler_params=pltpu.CompilerParams(vmem_limit_bytes=VMEM),
        name="spread",
    )(field, potential)
    return out.reshape(32 * 40, PLANE)


ROWS = 4 * NX
EDGE = 16
CHUNK = 256


def filter_kernel(in_ref, ring_ref, out_ref, one_ref, two_ref, diag_ref, sems):
    def fill(s, _):
        base = pl.multiple_of(s * 32, 32)
        one_ref[pl.ds(EDGE + base, 32), :] = in_ref[s, 0:32, :]
        pot = in_ref[s, 32:40, :]
        low = low_rows((8, PLANE))
        for t in range(4):
            row = jnp.where(low, pot[2 * t : 2 * t + 1], pot[2 * t + 1 : 2 * t + 2])
            diag_ref[pl.ds(base + 8 * t, 8), :] = 0.5 * row + 2.0 * DIAGONAL
        return 0

    lax.fori_loop(0, 32, fill, 0)
    ring = ring_ref[...]

    def close(ref):
        ref[0:EDGE, :] = ref[ROWS : ROWS + EDGE, :]
        ref[ROWS + EDGE :, :] = ref[EDGE : 2 * EDGE, :]

    def twice(cur_ref, base):
        wide = cur_ref[pl.ds(base, CHUNK + 2 * EDGE), :]
        cur = wide[EDGE : EDGE + CHUNK]
        near = dot(jnp.concatenate(split(cur), axis=1), ring)
        half = pltpu.roll(wide, 4, 0)

        def at(a, shift):
            return a[EDGE + shift : EDGE + shift + CHUNK]

        along = (
            STENCIL[0] * (at(half, 0) + at(half, 8))
            + STENCIL[1] * (at(wide, 8) + at(wide, -8))
            + (at(half, -8) + at(half, 16))
        )
        return (2.0 * UNIT) * (near + along) + diag_ref[pl.ds(base, CHUNK), :] * cur

    def sweep(body):
        for i in range(ROWS // CHUNK):
            body(i * CHUNK)

    def copy(ref, base):
        return pltpu.make_async_copy(
            ref.at[pl.ds(EDGE + base, CHUNK)],
            out_ref.at[pl.ds(base, CHUNK)],
            sems.at[base // CHUNK],
        )

    close(one_ref)

    def first(base):
        two_ref[pl.ds(EDGE + base, CHUNK), :] = 0.5 * twice(one_ref, base)

    sweep(first)
    previous, current = one_ref, two_ref
    for degree_step in range(2, DEGREE + 1):
        close(current)
        last = degree_step == DEGREE

        def following(base, previous=previous, current=current, last=last):
            rows = pl.ds(EDGE + base, CHUNK)
            previous[rows, :] = twice(current, base) - previous[rows, :]
            if last:
                copy(previous, base).start()

        sweep(following)
        previous, current = current, previous
    sweep(lambda base: copy(current, base).wait())


def chebyshev(spread_cells, ring):
    return pl.pallas_call(
        filter_kernel,
        out_shape=jax.ShapeDtypeStruct((ROWS, PLANE), F32),
        scratch_shapes=[
            pltpu.VMEM((ROWS + 2 * EDGE, PLANE), F32),
            pltpu.VMEM((ROWS + 2 * EDGE, PLANE), F32),
            pltpu.VMEM((ROWS, PLANE), F32),
            pltpu.SemaphoreType.DMA((ROWS // CHUNK,)),
        ],
        out_specs=pl.BlockSpec(memory_space=pltpu.HBM),
        compiler_params=pltpu.CompilerParams(vmem_limit_bytes=VMEM),
        name="chebyshev",
    )(spread_cells.reshape(32, 40, PLANE), ring)


BLOCKS = tuple((i, j) for i in range(4) for j in range(i, 4))
PART = 320


def gram_kernel(place_ref, in_ref, near_ref, far_ref, mine_ref, other_ref, cells_ref, sums_ref):
    for q in range(4):
        a = in_ref[:, 0, q]
        b = in_ref[:, 1, q]
        low = low_rows(a.shape)
        rows = pl.ds(128 * q, 128)
        cells_ref[rows, :PLANE] = jnp.where(low, a, swap_halves(b)).reshape(128, PLANE)
        cells_ref[rows, PLANE:] = jnp.where(low, swap_halves(a), b).reshape(128, PLANE)
    by_orbital = cells_ref[...]
    by_cell = by_orbital.T
    near_ref[...] = by_cell[:PART]
    far_ref[...] = by_cell[PART:]
    left, right = by_orbital.astype(BF16), split(by_cell)
    square, cross = dot(left, right[0]), dot(left, right[1])

    def block(a, i, j):
        return a[128 * i : 128 * (i + 1), 128 * j : 128 * (j + 1)]

    for k, (i, j) in enumerate(BLOCKS):
        rows = pl.ds(128 * (k % 5), 128)
        sums_ref[k // 5, rows, :] = block(square, i, j) + (
            block(cross, i, j) + block(cross, j, i).T
        )
    mine_ref[...] = sums_ref[place_ref[1]]
    other_ref[...] = sums_ref[1 - place_ref[1]]


SCALARS = pl.BlockSpec(memory_space=pltpu.SMEM)
VECTORS = pl.BlockSpec(memory_space=pltpu.VMEM)
ANYWHERE = pl.BlockSpec(memory_space=pl.ANY)


def gram(place, cells):
    return pl.pallas_call(
        gram_kernel,
        out_shape=(
            jax.ShapeDtypeStruct((PART, NORB), F32),
            jax.ShapeDtypeStruct((2 * PLANE - PART, NORB), F32),
            jax.ShapeDtypeStruct((640, 128), F32),
            jax.ShapeDtypeStruct((640, 128), F32),
        ),
        in_specs=[SCALARS, VECTORS],
        scratch_shapes=[pltpu.VMEM((NORB, 2 * PLANE), F32), pltpu.VMEM((2, 640, 128), F32)],
        compiler_params=pltpu.CompilerParams(vmem_limit_bytes=VMEM),
        name="gram",
    )(place, cells.reshape(16, 2, 4, 8, PLANE))


def product(a, b):
    top = dot3([p[:256] for p in a], b)
    low_block = dot_wide([p[256:] for p in a], [p[:, 256:] for p in b])
    return jnp.concatenate(
        [top, jnp.concatenate([top[:, 256:].T, low_block], axis=1)], axis=0
    )


def squared(a):
    cross = dot(a[0], a[1])
    return dot(a[0], a[0]) + (cross + cross.T)


def root_kernel(place_ref, mine_ref, other_ref, out_ref):
    zl, c = place_ref[0], place_ref[1]
    blocks = {}
    for k, (i, j) in enumerate(BLOCKS):
        rows = pl.ds(128 * (k % 5), 128)
        mine, other = mine_ref[rows, :], other_ref[rows, :]
        block = jnp.where(c == k // 5, mine, other) * (1.0 / (NX * PLANE))
        blocks[i, j] = block
        if i != j:
            blocks[j, i] = block.T
    total = jnp.concatenate(
        [jnp.concatenate([blocks[i, j] for j in range(4)], axis=1) for i in range(4)], axis=0
    )
    square = jnp.sum(jnp.sum(total * total, axis=0, keepdims=True), axis=1, keepdims=True)
    norm_scale = jnp.sqrt(square + 1e-06)
    row = lax.broadcasted_iota(jnp.int32, (NORB, NORB), 0)
    col = lax.broadcasted_iota(jnp.int32, (NORB, NORB), 1)
    diagonal = row == col
    m = total / norm_scale
    inverse = None
    for pair in range(NS_ITERS // 2):
        parts = split(m)
        m2 = squared(parts)
        tail = product(split(m2), split(0.0625 * m2 - 0.5625 * m))
        factor = (jnp.where(diagonal, 2.25, 0.0) - 2.4375 * m) + (1.6875 * m2 + tail)
        factors = split(factor)
        if inverse is None:
            chip = jnp.where(zl == 0, factor[:, :256], factor[:, 256:])
            first, second = chip[:, :128], chip[:, 128:]
            inverse = jnp.concatenate(
                [jnp.where(c == 0, first, second), jnp.where(c == 0, second, first)], axis=1
            )
        else:
            inverse = dot_wide(factors, split(inverse))
        if pair < NS_ITERS // 2 - 1:
            m = product(parts, split(squared(factors)))
    root = split(inverse / jnp.sqrt(norm_scale))
    out_ref[0] = root[0]
    out_ref[1] = root[1]


def inverse_root(place, mine, other):
    return pl.pallas_call(
        root_kernel,
        in_specs=[SCALARS, VECTORS, VECTORS],
        out_shape=jax.ShapeDtypeStruct((2, NORB, 256), BF16),
        compiler_params=pltpu.CompilerParams(vmem_limit_bytes=VMEM),
        name="inverse_root",
    )(place, mine, other)


def whiten_kernel(near_ref, far_ref, root_ref, ours_ref, theirs_ref):
    root = (root_ref[0], root_ref[1])
    for ref, rows in ((near_ref, pl.ds(0, PART)), (far_ref, pl.ds(PART, 2 * PLANE - PART))):
        white = dot_wide(split(ref[...]), root)
        ours_ref[rows, :] = white[:, :128]
        theirs_ref[rows, :] = white[:, 128:]


def whiten(near, far, root):
    return pl.pallas_call(
        whiten_kernel,
        out_shape=(jax.ShapeDtypeStruct((2 * PLANE, 128), F32),) * 2,
        compiler_params=pltpu.CompilerParams(vmem_limit_bytes=VMEM_SMALL),
        name="whiten",
    )(near, far, root)


WHOLE = jax.ShapeDtypeStruct((2, 2, 2 * PLANE, 128), F32)


def place_kernel(slots, place_ref, *refs):
    parts, whole_ref, sems = refs[: len(slots)], refs[-2], refs[-1]
    copies = []
    for k, (zl_flip, c_flip) in enumerate(slots):
        zl = 1 - place_ref[0] if zl_flip else place_ref[0]
        c = 1 - place_ref[1] if c_flip else place_ref[1]
        copies.append(pltpu.make_async_copy(parts[k], whole_ref.at[zl, c], sems.at[k]))
    for copy in copies:
        copy.start()
    for copy in copies:
        copy.wait()


def put(place, slots, parts, whole=None):
    aliased = () if whole is None else (whole,)
    return pl.pallas_call(
        functools.partial(place_kernel, slots),
        in_specs=[SCALARS] + [ANYWHERE] * (len(parts) + len(aliased)),
        out_specs=ANYWHERE,
        out_shape=WHOLE,
        scratch_shapes=[pltpu.SemaphoreType.DMA((len(parts),))],
        input_output_aliases={1 + len(parts): 0} if aliased else {},
        compiler_params=pltpu.CompilerParams(vmem_limit_bytes=VMEM_SMALL),
        name="put",
    )(place, *parts, *aliased)


def exchange(a, axes):
    return lax.all_to_all(a, axes, 0, 0, tiled=True)


def swap(a, axis):
    return lax.ppermute(a, axis, [(0, 1), (1, 0)])


def body(orbitals, potential):
    place = jnp.stack([lax.axis_index("zl"), lax.axis_index("c")])
    ring = jnp.asarray(np.tile(plane_stencil(), (2, 1)), BF16)
    sent = spread(orbitals.reshape(SLAB, PLANE, 128), potential)
    sent, place = lax.optimization_barrier((sent, place))
    filtered = chebyshev(exchange(sent, SPACE), ring)
    near, far, mine, other = gram(place, exchange(filtered, EVERY))

    other_near = swap(near, "zl")
    share = exchange(mine + swap(other, "c"), ("x", "y"))
    share = jnp.sum(share.reshape(16, -1, 128), axis=0)
    share, other_near = lax.optimization_barrier((share, other_near))
    share = share + swap(share, "zl")
    share = share + swap(share, "zh")
    share, far = lax.optimization_barrier((share, far))
    other_far = swap(far, "zl")
    total = exchange(jnp.tile(share, (16, 1)), ("x", "y"))
    root = inverse_root(place, total, swap(total, "c"))

    ours, theirs = whiten(near, far, root)
    first = swap(theirs, "c")
    other_ours, other_theirs = whiten(other_near, other_far, root)
    second = swap(other_theirs, "c")
    slots = ((False, False), (True, False), (False, True))
    whole = put(place, slots, (ours, other_ours, first))
    whitened = put(place, ((True, True),), (second,), whole)
    return whitened.reshape(orbitals.shape)


def solution(mesh):
    fine = Mesh(mesh.devices.reshape(4, 2, 4, 2, 2), EVERY)
    return jax.shard_map(
        body,
        mesh=fine,
        in_specs=(P(SPACE, None, None, ORB), P(SPACE, None, None)),
        out_specs=P(SPACE, None, None, ORB),
        check_vma=False,
    )
```

```python
import functools

import numpy as np
import jax
import jax.numpy as jnp
from jax import lax
from jax.experimental import pallas as pl
from jax.experimental.pallas import tpu as pltpu
from jax.sharding import Mesh, PartitionSpec as P

DEGREE = 4
NS_ITERS = 8
NY, NZ = 16, 32
PLANE = NY * NZ
NX = 256
NORB = 512
SLAB = 8
SPACE = ("x", "zh", "y")
ORB = ("zl", "c")
EVERY = SPACE + ORB
F32 = jnp.float32
BF16 = jnp.bfloat16
VMEM = 30 * 1024 * 1024
VMEM_SPREAD = 60 * 1024 * 1024
VMEM_SMALL = 24 * 1024 * 1024

STENCIL = (135.0, -13.5, 1.0)
UNIT = -0.5 / 90.0 / 4.0
DIAGONAL = (1.5 * 49.0 / 18.0 - 5.0) / 4.0


def plane_stencil():
    def ring(n):
        m = np.zeros((n, n), np.float32)
        for k, w in enumerate(STENCIL, 1):
            for i in range(n):
                m[i, (i + k) % n] += w
                m[i, (i - k) % n] += w
        return m

    return np.kron(ring(NY), np.eye(NZ, dtype=np.float32)) + np.kron(
        np.eye(NY, dtype=np.float32), ring(NZ)
    )


def low_rows(shape):
    return lax.broadcasted_iota(jnp.int32, shape, len(shape) - 2) < 4


def swap_halves(a):
    return pltpu.roll(a, 4, a.ndim - 2)


def split(a):
    hi = a.astype(BF16)
    return hi, (a - hi.astype(F32)).astype(BF16)


def dot(a, b):
    return jnp.dot(a, b, preferred_element_type=F32)


def dot_wide(a, b):
    wide = jnp.concatenate(b, axis=1)
    high, low = dot(a[0], wide), dot(a[1], wide)
    n = b[0].shape[1]
    return high[:, :n] + (high[:, n:] + low[:, :n])


def dot3(a, b):
    return dot(a[0], b[0]) + (dot(a[0], b[1]) + dot(a[1], b[0]))


def spread_kernel(v_hbm, pot_hbm, out_hbm, v_ref, pot_ref, out_ref, in_sems, out_sems):
    loads = [
        pltpu.make_async_copy(v_hbm.at[x], v_ref.at[x], in_sems.at[x]) for x in range(SLAB)
    ]
    loads.append(pltpu.make_async_copy(pot_hbm, pot_ref, in_sems.at[SLAB]))
    for load in loads:
        load.start()

    def store(t):
        rows = pl.ds(8 * t, 8)
        return pltpu.make_async_copy(
            out_ref.at[:, :, rows], out_hbm.at[:, :, rows], out_sems.at[t]
        )

    for t in range(4):
        loads[2 * t].wait()
        loads[2 * t + 1].wait()
        a = v_ref[2 * t].T.reshape(16, 8, PLANE)
        b = v_ref[2 * t + 1].T.reshape(16, 8, PLANE)
        low = low_rows(a.shape)
        rows = pl.ds(8 * t, 8)
        out_ref[:, 0, rows, :] = jnp.where(low, a, swap_halves(b))
        out_ref[:, 1, rows, :] = jnp.where(low, swap_halves(a), b)
        store(t).start()
        if t == 0:
            loads[SLAB].wait()
            pot = jnp.concatenate([pot_ref[:, y, :] for y in range(NY)], axis=1)
            out_ref[:, :, 32:40, :] = jnp.broadcast_to(pot, (16, 2, SLAB, PLANE))
            store(4).start()
    for t in range(5):
        store(t).wait()


def spread(field, potential):
    shape = (16, 2, 40, PLANE)
    out = pl.pallas_call(
        spread_kernel,
        in_specs=[pl.BlockSpec(memory_space=pl.ANY)] * 2,
        out_specs=pl.BlockSpec(memory_space=pl.ANY),
        out_shape=jax.ShapeDtypeStruct(shape, F32),
        scratch_shapes=[
            pltpu.VMEM((SLAB, PLANE, 128), F32),
            pltpu.VMEM((SLAB, NY, NZ), F32),
            pltpu.VMEM(shape, F32),
            pltpu.SemaphoreType.DMA((SLAB + 1,)),
            pltpu.SemaphoreType.DMA((5,)),
        ],
        compiler_params=pltpu.CompilerParams(vmem_limit_bytes=VMEM_SPREAD),
        name="spread",
    )(field, potential)
    return out.reshape(32 * 40, PLANE)


ROWS = 4 * NX
EDGE = 16
CHUNK = 256


def filter_kernel(in_ref, ring_ref, out_ref, one_ref, two_ref, diag_ref, sems):
    def fill(s, _):
        base = pl.multiple_of(s * 32, 32)
        one_ref[pl.ds(EDGE + base, 32), :] = in_ref[s, 0:32, :]
        pot = in_ref[s, 32:40, :]
        low = low_rows((8, PLANE))
        for t in range(4):
            row = jnp.where(low, pot[2 * t : 2 * t + 1], pot[2 * t + 1 : 2 * t + 2])
            diag_ref[pl.ds(base + 8 * t, 8), :] = 0.5 * row + 2.0 * DIAGONAL
        return 0

    lax.fori_loop(0, 32, fill, 0)
    ring = ring_ref[...]

    def close(ref):
        ref[0:EDGE, :] = ref[ROWS : ROWS + EDGE, :]
        ref[ROWS + EDGE :, :] = ref[EDGE : 2 * EDGE, :]

    def twice(cur_ref, base):
        wide = cur_ref[pl.ds(base, CHUNK + 2 * EDGE), :]
        cur = wide[EDGE : EDGE + CHUNK]
        near = dot(jnp.concatenate(split(cur), axis=1), ring)
        half = pltpu.roll(wide, 4, 0)

        def at(a, shift):
            return a[EDGE + shift : EDGE + shift + CHUNK]

        along = (
            STENCIL[0] * (at(half, 0) + at(half, 8))
            + STENCIL[1] * (at(wide, 8) + at(wide, -8))
            + (at(half, -8) + at(half, 16))
        )
        return (2.0 * UNIT) * (near + along) + diag_ref[pl.ds(base, CHUNK), :] * cur

    def sweep(body):
        for i in range(ROWS // CHUNK):
            body(i * CHUNK)

    def copy(ref, base):
        return pltpu.make_async_copy(
            ref.at[pl.ds(EDGE + base, CHUNK)],
            out_ref.at[pl.ds(base, CHUNK)],
            sems.at[base // CHUNK],
        )

    close(one_ref)

    def first(base):
        two_ref[pl.ds(EDGE + base, CHUNK), :] = 0.5 * twice(one_ref, base)

    sweep(first)
    previous, current = one_ref, two_ref
    for degree_step in range(2, DEGREE + 1):
        close(current)
        last = degree_step == DEGREE

        def following(base, previous=previous, current=current, last=last):
            rows = pl.ds(EDGE + base, CHUNK)
            previous[rows, :] = twice(current, base) - previous[rows, :]
            if last:
                copy(previous, base).start()

        sweep(following)
        previous, current = current, previous
    sweep(lambda base: copy(current, base).wait())


def chebyshev(spread_cells, ring):
    return pl.pallas_call(
        filter_kernel,
        out_shape=jax.ShapeDtypeStruct((ROWS, PLANE), F32),
        scratch_shapes=[
            pltpu.VMEM((ROWS + 2 * EDGE, PLANE), F32),
            pltpu.VMEM((ROWS + 2 * EDGE, PLANE), F32),
            pltpu.VMEM((ROWS, PLANE), F32),
            pltpu.SemaphoreType.DMA((ROWS // CHUNK,)),
        ],
        out_specs=pl.BlockSpec(memory_space=pltpu.HBM),
        compiler_params=pltpu.CompilerParams(vmem_limit_bytes=VMEM),
        name="chebyshev",
    )(spread_cells.reshape(32, 40, PLANE), ring)


BLOCKS = tuple((i, j) for i in range(4) for j in range(i, 4))
PART = 352


def turn_kernel(in_ref, near_ref, far_ref, left_ref, cells_ref):
    for q in range(4):
        a = in_ref[:, 0, q]
        b = in_ref[:, 1, q]
        low = low_rows(a.shape)
        rows = pl.ds(128 * q, 128)
        cells_ref[rows, :PLANE] = jnp.where(low, a, swap_halves(b)).reshape(128, PLANE)
        cells_ref[rows, PLANE:] = jnp.where(low, swap_halves(a), b).reshape(128, PLANE)
    by_orbital = cells_ref[...]
    by_cell = by_orbital.T
    near_ref[...] = by_cell[:PART]
    far_ref[...] = by_cell[PART:]
    left_ref[...] = by_orbital.astype(BF16)


def turn(cells):
    return pl.pallas_call(
        turn_kernel,
        out_shape=(
            jax.ShapeDtypeStruct((PART, NORB), F32),
            jax.ShapeDtypeStruct((2 * PLANE - PART, NORB), F32),
            jax.ShapeDtypeStruct((NORB, 2 * PLANE), BF16),
        ),
        scratch_shapes=[pltpu.VMEM((NORB, 2 * PLANE), F32)],
        compiler_params=pltpu.CompilerParams(vmem_limit_bytes=VMEM_SMALL),
        name="turn",
    )(cells.reshape(16, 2, 4, 8, PLANE))


def gram_kernel(place_ref, near_ref, far_ref, left_ref, mine_ref, other_ref, sums_ref):
    right = split(jnp.concatenate([near_ref[...], far_ref[...]], axis=0))
    square, cross = dot(left_ref[...], right[0]), dot(left_ref[...], right[1])

    def block(a, i, j):
        return a[128 * i : 128 * (i + 1), 128 * j : 128 * (j + 1)]

    for k, (i, j) in enumerate(BLOCKS):
        rows = pl.ds(128 * (k % 5), 128)
        sums_ref[k // 5, rows, :] = block(square, i, j) + (
            block(cross, i, j) + block(cross, j, i).T
        )
    mine_ref[...] = sums_ref[place_ref[1]]
    other_ref[...] = sums_ref[1 - place_ref[1]]


SCALARS = pl.BlockSpec(memory_space=pltpu.SMEM)
VECTORS = pl.BlockSpec(memory_space=pltpu.VMEM)
ANYWHERE = pl.BlockSpec(memory_space=pl.ANY)


def gram(place, near, far, left):
    return pl.pallas_call(
        gram_kernel,
        in_specs=[SCALARS, VECTORS, VECTORS, VECTORS],
        out_shape=(jax.ShapeDtypeStruct((640, 128), F32),) * 2,
        scratch_shapes=[pltpu.VMEM((2, 640, 128), F32)],
        compiler_params=pltpu.CompilerParams(vmem_limit_bytes=VMEM_SMALL),
        name="gram",
    )(place, near, far, left)


def mirrored(a):
    row = lax.broadcasted_iota(jnp.int32, a.shape, 0)
    col = lax.broadcasted_iota(jnp.int32, a.shape, 1)
    return jnp.where(row <= col, a, a.T)


def product(a, b):
    top = dot3([p[:256] for p in a], b)
    low_block = dot_wide([p[256:] for p in a], [p[:, 256:] for p in b])
    return jnp.concatenate(
        [
            jnp.concatenate([mirrored(top[:, :256]), top[:, 256:]], axis=1),
            jnp.concatenate([top[:, 256:].T, mirrored(low_block)], axis=1),
        ],
        axis=0,
    )


def squared(a):
    cross = dot(a[0], a[1])
    return dot(a[0], a[0]) + (cross + cross.T)


def root_kernel(place_ref, mine_ref, other_ref, out_ref):
    zl, c = place_ref[0], place_ref[1]
    blocks = {}
    for k, (i, j) in enumerate(BLOCKS):
        rows = pl.ds(128 * (k % 5), 128)
        mine, other = mine_ref[rows, :], other_ref[rows, :]
        block = jnp.where(c == k // 5, mine, other) * (1.0 / (NX * PLANE))
        blocks[i, j] = block
        if i != j:
            blocks[j, i] = block.T
    total = jnp.concatenate(
        [jnp.concatenate([blocks[i, j] for j in range(4)], axis=1) for i in range(4)], axis=0
    )
    square = jnp.sum(jnp.sum(total * total, axis=0, keepdims=True), axis=1, keepdims=True)
    norm_scale = jnp.sqrt(square + 1e-06)
    row = lax.broadcasted_iota(jnp.int32, (NORB, NORB), 0)
    col = lax.broadcasted_iota(jnp.int32, (NORB, NORB), 1)
    diagonal = row == col
    m = total / norm_scale
    inverse = None
    for pair in range(NS_ITERS // 2):
        parts = split(m)
        m2 = squared(parts)
        base = 0.25 * m2 - 1.125 * m + jnp.where(diagonal, 27.0 / 32.0, 0.0)
        rest = jnp.where(diagonal, 1575.0 / 1024.0, 0.0) - (69.0 / 128.0) * m
        factor = squared(split(base)) + rest
        factors = split(factor)
        if inverse is None:
            chip = jnp.where(zl == 0, factor[:, :256], factor[:, 256:])
            first, second = chip[:, :128], chip[:, 128:]
            inverse = jnp.concatenate(
                [jnp.where(c == 0, first, second), jnp.where(c == 0, second, first)], axis=1
            )
        else:
            inverse = dot_wide(factors, split(inverse))
        if pair < NS_ITERS // 2 - 1:
            m = product(parts, split(squared(factors)))
    root = split(inverse / jnp.sqrt(norm_scale))
    out_ref[0] = root[0]
    out_ref[1] = root[1]


def inverse_root(place, mine, other):
    return pl.pallas_call(
        root_kernel,
        in_specs=[SCALARS, VECTORS, VECTORS],
        out_shape=jax.ShapeDtypeStruct((2, NORB, 256), BF16),
        compiler_params=pltpu.CompilerParams(vmem_limit_bytes=VMEM),
        name="inverse_root",
    )(place, mine, other)


def whiten_kernel(near_ref, far_ref, root_ref, ours_ref, theirs_ref):
    root = (root_ref[0], root_ref[1])
    for ref, rows in ((near_ref, pl.ds(0, PART)), (far_ref, pl.ds(PART, 2 * PLANE - PART))):
        white = dot_wide(split(ref[...]), root)
        ours_ref[rows, :] = white[:, :128]
        theirs_ref[rows, :] = white[:, 128:]


def whiten(near, far, root):
    return pl.pallas_call(
        whiten_kernel,
        out_shape=(jax.ShapeDtypeStruct((2 * PLANE, 128), F32),) * 2,
        compiler_params=pltpu.CompilerParams(vmem_limit_bytes=VMEM_SMALL),
        name="whiten",
    )(near, far, root)


WHOLE = jax.ShapeDtypeStruct((2, 2, 2 * PLANE, 128), F32)


def place_kernel(slots, place_ref, *refs):
    parts, whole_ref, sems = refs[: len(slots)], refs[-2], refs[-1]
    copies = []
    for k, (zl_flip, c_flip) in enumerate(slots):
        zl = 1 - place_ref[0] if zl_flip else place_ref[0]
        c = 1 - place_ref[1] if c_flip else place_ref[1]
        copies.append(pltpu.make_async_copy(parts[k], whole_ref.at[zl, c], sems.at[k]))
    for copy in copies:
        copy.start()
    for copy in copies:
        copy.wait()


def put(place, slots, parts, whole=None):
    aliased = () if whole is None else (whole,)
    return pl.pallas_call(
        functools.partial(place_kernel, slots),
        in_specs=[SCALARS] + [ANYWHERE] * (len(parts) + len(aliased)),
        out_specs=ANYWHERE,
        out_shape=WHOLE,
        scratch_shapes=[pltpu.SemaphoreType.DMA((len(parts),))],
        input_output_aliases={1 + len(parts): 0} if aliased else {},
        compiler_params=pltpu.CompilerParams(vmem_limit_bytes=VMEM_SMALL),
        name="put",
    )(place, *parts, *aliased)


def exchange(a, axes):
    return lax.all_to_all(a, axes, 0, 0, tiled=True)


def swap(a, axis):
    return lax.ppermute(a, axis, [(0, 1), (1, 0)])


def body(orbitals, potential):
    place = jnp.stack([lax.axis_index("zl"), lax.axis_index("c")])
    ring = jnp.asarray(np.tile(plane_stencil(), (2, 1)), BF16)
    sent = spread(orbitals.reshape(SLAB, PLANE, 128), potential)
    sent, place = lax.optimization_barrier((sent, place))
    filtered = chebyshev(exchange(sent, SPACE), ring)
    near, far, left = turn(exchange(filtered, EVERY))
    mine, other = gram(place, near, far, left)

    other_near = swap(near, "zl")
    share = exchange(mine + swap(other, "c"), ("x", "y"))
    share = jnp.sum(share.reshape(16, -1, 128), axis=0)
    share, other_near = lax.optimization_barrier((share, other_near))
    ring_z = [
        lax.ppermute(share, ("zh", "zl"), [(i, (i + k) % 4) for i in range(4)]) for k in (2, 1, 3)
    ]
    share = (share + ring_z[0]) + (ring_z[1] + ring_z[2])
    share, far = lax.optimization_barrier((share, far))
    other_far = swap(far, "zl")
    total = exchange(jnp.tile(share, (16, 1)), ("x", "y"))
    root = inverse_root(place, total, swap(total, "c"))

    ours, theirs = whiten(near, far, root)
    first = swap(theirs, "c")
    other_ours, other_theirs = whiten(other_near, other_far, root)
    second = swap(other_theirs, "c")
    slots = ((False, False), (True, False), (False, True))
    whole = put(place, slots, (ours, other_ours, first))
    whitened = put(place, ((True, True),), (second,), whole)
    return whitened.reshape(orbitals.shape)


def solution(mesh):
    fine = Mesh(mesh.devices.reshape(4, 2, 4, 2, 2), EVERY)
    return jax.shard_map(
        body,
        mesh=fine,
        in_specs=(P(SPACE, None, None, ORB), P(SPACE, None, None)),
        out_specs=P(SPACE, None, None, ORB),
        check_vma=False,
    )
```

```python
import functools

import numpy as np
import jax
import jax.numpy as jnp
from jax import lax
from jax.experimental import pallas as pl
from jax.experimental.pallas import tpu as pltpu
from jax.sharding import Mesh, PartitionSpec as P

DEGREE = 4
NS_ITERS = 8
NY, NZ = 16, 32
PLANE = NY * NZ
NX = 256
NORB = 512
SLAB = 8
SPACE = ("x", "zh", "y")
ORB = ("zl", "c")
EVERY = SPACE + ORB
F32 = jnp.float32
BF16 = jnp.bfloat16
VMEM = 30 * 1024 * 1024
VMEM_SPREAD = 60 * 1024 * 1024
VMEM_SMALL = 24 * 1024 * 1024

STENCIL = (135.0, -13.5, 1.0)
UNIT = -0.5 / 90.0 / 4.0
DIAGONAL = (1.5 * 49.0 / 18.0 - 5.0) / 4.0


def plane_stencil():
    def ring(n):
        m = np.zeros((n, n), np.float32)
        for k, w in enumerate(STENCIL, 1):
            for i in range(n):
                m[i, (i + k) % n] += w
                m[i, (i - k) % n] += w
        return m

    return np.kron(ring(NY), np.eye(NZ, dtype=np.float32)) + np.kron(
        np.eye(NY, dtype=np.float32), ring(NZ)
    )


def low_rows(shape):
    return lax.broadcasted_iota(jnp.int32, shape, len(shape) - 2) < 4


def swap_halves(a):
    return pltpu.roll(a, 4, a.ndim - 2)


def split(a):
    hi = a.astype(BF16)
    return hi, (a - hi.astype(F32)).astype(BF16)


def dot(a, b):
    return jnp.dot(a, b, preferred_element_type=F32)


def dot_wide(a, b):
    wide = jnp.concatenate(b, axis=1)
    high, low = dot(a[0], wide), dot(a[1], wide)
    n = b[0].shape[1]
    return high[:, :n] + (high[:, n:] + low[:, :n])


def dot3(a, b):
    return dot(a[0], b[0]) + (dot(a[0], b[1]) + dot(a[1], b[0]))


FIELD_ROWS = 128
POT_ROWS = 16
MESSAGE = FIELD_ROWS + POT_ROWS


def spread_kernel(v_hbm, pot_hbm, out_hbm, v_ref, pot_ref, out_ref, in_sems, out_sems):
    pot_load = pltpu.make_async_copy(pot_hbm, pot_ref, in_sems.at[SLAB])
    pot_load.start()
    loads = [
        pltpu.make_async_copy(v_hbm.at[x], v_ref.at[x], in_sems.at[x]) for x in range(SLAB)
    ]
    for load in loads:
        load.start()

    def store(t):
        rows = pl.ds(32 * t, 32 if t < 4 else POT_ROWS)
        return pltpu.make_async_copy(
            out_ref.at[:, :, rows], out_hbm.at[:, :, rows], out_sems.at[t]
        )

    pot_load.wait()
    pot = jnp.concatenate([pot_ref[:, y, :] for y in range(NY)], axis=1)
    half = jnp.where(lax.axis_index("c") == 0, pot[:4], pot[4:])
    for k in range(2):
        tile = jnp.concatenate(
            [half[:, 256 * k + 128 * u : 256 * k + 128 * (u + 1)] for u in range(2)], axis=0
        )
        rows = pl.ds(FIELD_ROWS + 8 * k, 8)
        out_ref[:, :, rows, :] = jnp.broadcast_to(tile, (16, 2, 8, 128))
    store(4).start()
    for t in range(4):
        loads[2 * t].wait()
        loads[2 * t + 1].wait()
        a = v_ref[2 * t].T.reshape(16, 8, PLANE)
        b = v_ref[2 * t + 1].T.reshape(16, 8, PLANE)
        low = low_rows(a.shape)
        even = jnp.where(low, a, swap_halves(b))
        odd = jnp.where(low, swap_halves(a), b)
        for k in range(4):
            rows, lanes = pl.ds(32 * t + 8 * k, 8), slice(128 * k, 128 * (k + 1))
            out_ref[:, 0, rows, :] = even[:, :, lanes]
            out_ref[:, 1, rows, :] = odd[:, :, lanes]
        store(t).start()
    for t in range(5):
        store(t).wait()


def spread(field, potential):
    shape = (16, 2, MESSAGE, 128)
    out = pl.pallas_call(
        spread_kernel,
        in_specs=[pl.BlockSpec(memory_space=pl.ANY)] * 2,
        out_specs=pl.BlockSpec(memory_space=pl.ANY),
        out_shape=jax.ShapeDtypeStruct(shape, F32),
        scratch_shapes=[
            pltpu.VMEM((SLAB, PLANE, 128), F32),
            pltpu.VMEM((SLAB, NY, NZ), F32),
            pltpu.VMEM(shape, F32),
            pltpu.SemaphoreType.DMA((SLAB + 1,)),
            pltpu.SemaphoreType.DMA((5,)),
        ],
        compiler_params=pltpu.CompilerParams(vmem_limit_bytes=VMEM_SPREAD),
        name="spread",
    )(field, potential)
    return out.reshape(32 * MESSAGE, 128)


ROWS = 4 * NX
EDGE = 16
CHUNK = 256


CHUNKS = ROWS // CHUNK
PARTS = 32 // CHUNKS


def neighbours(wide, ring):
    near = dot(jnp.concatenate(split(wide[EDGE : EDGE + CHUNK]), axis=1), ring)
    half = pltpu.roll(wide, 4, 0)

    def at(a, shift):
        return a[EDGE + shift : EDGE + shift + CHUNK]

    along = (
        STENCIL[0] * (at(half, 0) + at(half, 8))
        + STENCIL[1] * (at(wide, 8) + at(wide, -8))
        + (at(half, -8) + at(half, 16))
    )
    return near + along


def gather_kernel(in_ref, ring_ref, field_ref, sum_ref):
    def planes(s, first, count):
        tiles = in_ref[s, 32 * first : 32 * (first + count), :].reshape(-1, count, 4, 8, 128)
        return jnp.concatenate(
            [tiles[:, :, k].reshape(-1, 128) for k in range(4)], axis=1
        )

    ring = ring_ref[...]
    for i in range(CHUNKS):
        before, after = (PARTS * i - 1) % 32, PARTS * (i + 1) % 32
        middle = planes(slice(PARTS * i, PARTS * (i + 1)), 0, 4)
        wide = jnp.concatenate(
            [
                planes(slice(before, before + 1), 2, 2),
                middle,
                planes(slice(after, after + 1), 0, 2),
            ],
            axis=0,
        )
        rows = pl.ds(CHUNK * i, CHUNK)
        field_ref[rows, :] = middle
        sum_ref[rows, :] = neighbours(wide, ring)


def gather(messages, ring):
    return pl.pallas_call(
        gather_kernel,
        out_shape=(jax.ShapeDtypeStruct((ROWS, PLANE), F32),) * 2,
        compiler_params=pltpu.CompilerParams(vmem_limit_bytes=VMEM),
        name="gather",
    )(messages, ring)


def filter_kernel(
    place_ref, field_ref, sum_ref, mine_ref, other_ref, ring_ref,
    out_ref, one_ref, two_ref, diag_ref, sems,
):
    c = place_ref[1]

    def fill(s, _):
        base = pl.multiple_of(s * 32, 32)
        mine, other = mine_ref[s], other_ref[s]
        low = low_rows((8, 128))
        for h in range(2):
            pot = 0.5 * jnp.where(c == h, mine, other) + 2.0 * DIAGONAL
            for t in range(2):
                tiles = []
                for k in range(4):
                    at = 8 * (k // 2) + 4 * (k % 2) + 2 * t
                    tiles.append(jnp.where(low, pot[at : at + 1], pot[at + 1 : at + 2]))
                diag = jnp.concatenate(tiles, axis=1)
                at = base + 16 * h + 8 * t
                rows = pl.ds(at, 8)
                diag_ref[rows, :] = diag
                one_ref[pl.ds(EDGE + at, 8), :] = (
                    UNIT * sum_ref[rows, :] + 0.5 * diag * field_ref[rows, :]
                )
        return 0

    lax.fori_loop(0, 32, fill, 0, unroll=4)
    ring = ring_ref[...]

    def close(ref):
        ref[0:EDGE, :] = ref[ROWS : ROWS + EDGE, :]
        ref[ROWS + EDGE :, :] = ref[EDGE : 2 * EDGE, :]

    def twice(cur_ref, base):
        wide = cur_ref[pl.ds(base, CHUNK + 2 * EDGE), :]
        cur = wide[EDGE : EDGE + CHUNK]
        return (2.0 * UNIT) * neighbours(wide, ring) + diag_ref[pl.ds(base, CHUNK), :] * cur

    def copy(base):
        return pltpu.make_async_copy(
            two_ref.at[pl.ds(EDGE + base, CHUNK)],
            out_ref.at[pl.ds(base, CHUNK)],
            sems.at[base // CHUNK],
        )

    def sweep(body):
        for i in range(CHUNKS):
            body(i * CHUNK)

    def second(base):
        two_ref[pl.ds(EDGE + base, CHUNK), :] = (
            twice(one_ref, base) - field_ref[pl.ds(base, CHUNK), :]
        )

    def third(base):
        rows = pl.ds(EDGE + base, CHUNK)
        one_ref[rows, :] = twice(two_ref, base) - one_ref[rows, :]

    def fourth(base):
        rows = pl.ds(EDGE + base, CHUNK)
        two_ref[rows, :] = twice(one_ref, base) - two_ref[rows, :]
        copy(base).start()

    close(one_ref)
    for body, ref in ((second, two_ref), (third, one_ref)):
        sweep(body)
        close(ref)
    sweep(fourth)
    sweep(lambda base: copy(base).wait())


def chebyshev(place, field, partial_sum, mine, other, ring):
    smem = pl.BlockSpec(memory_space=pltpu.SMEM)
    vmem = pl.BlockSpec(memory_space=pltpu.VMEM)
    return pl.pallas_call(
        filter_kernel,
        in_specs=[smem] + [vmem] * 5,
        out_shape=jax.ShapeDtypeStruct((ROWS, PLANE), F32),
        scratch_shapes=[
            pltpu.VMEM((ROWS + 2 * EDGE, PLANE), F32),
            pltpu.VMEM((ROWS + 2 * EDGE, PLANE), F32),
            pltpu.VMEM((ROWS, PLANE), F32),
            pltpu.SemaphoreType.DMA((CHUNKS,)),
        ],
        out_specs=pl.BlockSpec(memory_space=pltpu.HBM),
        compiler_params=pltpu.CompilerParams(vmem_limit_bytes=VMEM),
        name="chebyshev",
    )(place, field, partial_sum, mine, other, ring)


BLOCKS = tuple((i, j) for i in range(4) for j in range(i, 4))
PART = 352


def turn_kernel(in_ref, near_ref, far_ref, left_ref, cells_ref):
    for q in range(4):
        a = in_ref[:, 0, q]
        b = in_ref[:, 1, q]
        low = low_rows(a.shape)
        rows = pl.ds(128 * q, 128)
        cells_ref[rows, :PLANE] = jnp.where(low, a, swap_halves(b)).reshape(128, PLANE)
        cells_ref[rows, PLANE:] = jnp.where(low, swap_halves(a), b).reshape(128, PLANE)
    by_orbital = cells_ref[...]
    by_cell = by_orbital.T
    near_ref[...] = by_cell[:PART]
    far_ref[...] = by_cell[PART:]
    left_ref[...] = by_orbital.astype(BF16)


def turn(cells):
    return pl.pallas_call(
        turn_kernel,
        out_shape=(
            jax.ShapeDtypeStruct((PART, NORB), F32),
            jax.ShapeDtypeStruct((2 * PLANE - PART, NORB), F32),
            jax.ShapeDtypeStruct((NORB, 2 * PLANE), BF16),
        ),
        scratch_shapes=[pltpu.VMEM((NORB, 2 * PLANE), F32)],
        compiler_params=pltpu.CompilerParams(vmem_limit_bytes=VMEM_SMALL),
        name="turn",
    )(cells.reshape(16, 2, 4, 8, PLANE))


def gram_kernel(place_ref, near_ref, far_ref, left_ref, mine_ref, other_ref, sums_ref):
    right = split(jnp.concatenate([near_ref[...], far_ref[...]], axis=0))
    square, cross = dot(left_ref[...], right[0]), dot(left_ref[...], right[1])

    def block(a, i, j):
        return a[128 * i : 128 * (i + 1), 128 * j : 128 * (j + 1)]

    for k, (i, j) in enumerate(BLOCKS):
        rows = pl.ds(128 * (k % 5), 128)
        sums_ref[k // 5, rows, :] = block(square, i, j) + (
            block(cross, i, j) + block(cross, j, i).T
        )
    mine_ref[...] = sums_ref[place_ref[1]]
    other_ref[...] = sums_ref[1 - place_ref[1]]


SCALARS = pl.BlockSpec(memory_space=pltpu.SMEM)
VECTORS = pl.BlockSpec(memory_space=pltpu.VMEM)
ANYWHERE = pl.BlockSpec(memory_space=pl.ANY)


def gram(place, near, far, left):
    return pl.pallas_call(
        gram_kernel,
        in_specs=[SCALARS, VECTORS, VECTORS, VECTORS],
        out_shape=(jax.ShapeDtypeStruct((640, 128), F32),) * 2,
        scratch_shapes=[pltpu.VMEM((2, 640, 128), F32)],
        compiler_params=pltpu.CompilerParams(vmem_limit_bytes=VMEM_SMALL),
        name="gram",
    )(place, near, far, left)


def mirrored(a):
    row = lax.broadcasted_iota(jnp.int32, a.shape, 0)
    col = lax.broadcasted_iota(jnp.int32, a.shape, 1)
    return jnp.where(row <= col, a, a.T)


def product(a, b):
    top = dot3([p[:256] for p in a], b)
    low_block = dot_wide([p[256:] for p in a], [p[:, 256:] for p in b])
    return jnp.concatenate(
        [
            jnp.concatenate([mirrored(top[:, :256]), top[:, 256:]], axis=1),
            jnp.concatenate([top[:, 256:].T, mirrored(low_block)], axis=1),
        ],
        axis=0,
    )


def squared(a):
    cross = dot(a[0], a[1])
    return dot(a[0], a[0]) + (cross + cross.T)


def root_kernel(place_ref, mine_ref, other_ref, out_ref):
    zl, c = place_ref[0], place_ref[1]
    blocks = {}
    for k, (i, j) in enumerate(BLOCKS):
        rows = pl.ds(128 * (k % 5), 128)
        mine, other = mine_ref[rows, :], other_ref[rows, :]
        block = jnp.where(c == k // 5, mine, other) * (1.0 / (NX * PLANE))
        blocks[i, j] = block
        if i != j:
            blocks[j, i] = block.T
    total = jnp.concatenate(
        [jnp.concatenate([blocks[i, j] for j in range(4)], axis=1) for i in range(4)], axis=0
    )
    square = jnp.sum(jnp.sum(total * total, axis=0, keepdims=True), axis=1, keepdims=True)
    norm_scale = jnp.sqrt(square + 1e-06)
    row = lax.broadcasted_iota(jnp.int32, (NORB, NORB), 0)
    col = lax.broadcasted_iota(jnp.int32, (NORB, NORB), 1)
    diagonal = row == col
    m = total / norm_scale
    inverse = None
    for pair in range(NS_ITERS // 2):
        parts = split(m)
        m2 = squared(parts)
        base = 0.25 * m2 - 1.125 * m + jnp.where(diagonal, 27.0 / 32.0, 0.0)
        rest = jnp.where(diagonal, 1575.0 / 1024.0, 0.0) - (69.0 / 128.0) * m
        factor = squared(split(base)) + rest
        factors = split(factor)
        if inverse is None:
            chip = jnp.where(zl == 0, factor[:, :256], factor[:, 256:])
            first, second = chip[:, :128], chip[:, 128:]
            inverse = jnp.concatenate(
                [jnp.where(c == 0, first, second), jnp.where(c == 0, second, first)], axis=1
            )
        else:
            inverse = dot_wide(factors, split(inverse))
        if pair < NS_ITERS // 2 - 1:
            m = product(parts, split(squared(factors)))
    root = split(inverse / jnp.sqrt(norm_scale))
    out_ref[0] = root[0]
    out_ref[1] = root[1]


def inverse_root(place, mine, other):
    return pl.pallas_call(
        root_kernel,
        in_specs=[SCALARS, VECTORS, VECTORS],
        out_shape=jax.ShapeDtypeStruct((2, NORB, 256), BF16),
        compiler_params=pltpu.CompilerParams(vmem_limit_bytes=VMEM),
        name="inverse_root",
    )(place, mine, other)


def whiten_kernel(*refs):
    chunks, root_ref, ours_ref, theirs_ref = refs[:-3], refs[-3], refs[-2], refs[-1]
    root = (root_ref[0], root_ref[1])
    start = 0
    for ref in chunks:
        white = dot_wide(split(ref[...]), root)
        rows = pl.ds(start, ref.shape[0])
        ours_ref[rows, :] = white[:, :128]
        theirs_ref[rows, :] = white[:, 128:]
        start += ref.shape[0]


def whiten(chunks, root):
    rows = sum(chunk.shape[0] for chunk in chunks)
    return pl.pallas_call(
        whiten_kernel,
        out_shape=(jax.ShapeDtypeStruct((rows, 128), F32),) * 2,
        compiler_params=pltpu.CompilerParams(vmem_limit_bytes=VMEM_SMALL),
        name="whiten",
    )(*chunks, root)


WHOLE = jax.ShapeDtypeStruct((2, 2, 2 * PLANE, 128), F32)


def place_kernel(jobs, place_ref, *refs):
    whole_ref, sems = refs[-2], refs[-1]
    copies = []
    for k, (part, source, rows, other_chip, other_core, at) in enumerate(jobs):
        zl = 1 - place_ref[0] if other_chip else place_ref[0]
        c = 1 - place_ref[1] if other_core else place_ref[1]
        copies.append(
            pltpu.make_async_copy(
                refs[part].at[pl.ds(source, rows)],
                whole_ref.at[zl, c, pl.ds(at, rows)],
                sems.at[k],
            )
        )
    for copy in copies:
        copy.start()
    for copy in copies:
        copy.wait()


def put(place, jobs, parts, whole=None):
    aliased = () if whole is None else (whole,)
    return pl.pallas_call(
        functools.partial(place_kernel, jobs),
        in_specs=[SCALARS] + [ANYWHERE] * (len(parts) + len(aliased)),
        out_specs=ANYWHERE,
        out_shape=WHOLE,
        scratch_shapes=[pltpu.SemaphoreType.DMA((len(jobs),))],
        input_output_aliases={1 + len(parts): 0} if aliased else {},
        compiler_params=pltpu.CompilerParams(vmem_limit_bytes=VMEM_SMALL),
        name="put",
    )(place, *parts, *aliased)


def exchange(a, axes):
    return lax.all_to_all(a, axes, 0, 0, tiled=True)


def swap(a, axis):
    return lax.ppermute(a, axis, [(0, 1), (1, 0)])


def body(orbitals, potential):
    place = jnp.stack([lax.axis_index("zl"), lax.axis_index("c")])
    ring = jnp.asarray(np.tile(plane_stencil(), (2, 1)), BF16)
    sent = spread(orbitals.reshape(SLAB, PLANE, 128), potential)
    sent, place = lax.optimization_barrier((sent, place))
    messages = exchange(sent, SPACE).reshape(32, MESSAGE, 128)
    half = messages[:, FIELD_ROWS:]
    other_half = swap(half, "c")
    field, partial_sum = gather(messages, ring)
    filtered = chebyshev(place, field, partial_sum, half, other_half, ring)
    near, far, left = turn(exchange(filtered, EVERY))
    mine, other = gram(place, near, far, left)

    other_near = swap(near, "zl")
    share = exchange(mine + swap(other, "c"), ("x", "y"))
    share = jnp.sum(share.reshape(16, -1, 128), axis=0)
    share, other_near = lax.optimization_barrier((share, other_near))
    ring_z = [
        lax.ppermute(share, ("zh", "zl"), [(i, (i + k) % 4) for i in range(4)]) for k in (2, 1, 3)
    ]
    share = (share + ring_z[0]) + (ring_z[1] + ring_z[2])
    share, far = lax.optimization_barrier((share, far))
    other_far = swap(far, "zl")
    total = exchange(jnp.tile(share, (16, 1)), ("x", "y"))
    root = inverse_root(place, total, swap(total, "c"))

    ours, theirs = whiten((near, far, other_near), root)
    first = swap(theirs, "c")
    late_ours, late_theirs = whiten((other_far,), root)
    second = swap(late_theirs, "c")
    chunk, late = 2 * PLANE, 2 * PLANE - PART
    jobs = tuple(
        job
        for part, other_core in ((0, False), (2, True))
        for job in (
            (part, 0, chunk, False, other_core, 0),
            (part, chunk, PART, True, other_core, 0),
        )
    )
    whole = put(place, jobs + ((1, 0, late, True, False, PART),), (ours, late_ours, first))
    whitened = put(place, ((0, 0, late, True, True, PART),), (second,), whole)
    return whitened.reshape(orbitals.shape)


def solution(mesh):
    fine = Mesh(mesh.devices.reshape(4, 2, 4, 2, 2), EVERY)
    return jax.shard_map(
        body,
        mesh=fine,
        in_specs=(P(SPACE, None, None, ORB), P(SPACE, None, None)),
        out_specs=P(SPACE, None, None, ORB),
        check_vma=False,
    )
```

```python
import functools

import numpy as np
import jax
import jax.numpy as jnp
from jax import lax
from jax.experimental import pallas as pl
from jax.experimental.pallas import tpu as pltpu
from jax.sharding import Mesh, PartitionSpec as P

DEGREE = 4
NS_ITERS = 8
NY, NZ = 16, 32
PLANE = NY * NZ
NX = 256
NORB = 512
SLAB = 8
SPACE = ("x", "zh", "y")
ORB = ("zl", "c")
EVERY = SPACE + ORB
F32 = jnp.float32
BF16 = jnp.bfloat16
VMEM = 30 * 1024 * 1024
VMEM_SPREAD = 60 * 1024 * 1024
VMEM_SMALL = 24 * 1024 * 1024

STENCIL = (135.0, -13.5, 1.0)
UNIT = -0.5 / 90.0 / 4.0
DIAGONAL = (1.5 * 49.0 / 18.0 - 5.0) / 4.0


def plane_stencil():
    def ring(n):
        m = np.zeros((n, n), np.float32)
        for k, w in enumerate(STENCIL, 1):
            for i in range(n):
                m[i, (i + k) % n] += w
                m[i, (i - k) % n] += w
        return m

    return np.kron(ring(NY), np.eye(NZ, dtype=np.float32)) + np.kron(
        np.eye(NY, dtype=np.float32), ring(NZ)
    )


def low_rows(shape):
    return lax.broadcasted_iota(jnp.int32, shape, len(shape) - 2) < 4


def swap_halves(a):
    return pltpu.roll(a, 4, a.ndim - 2)


def split(a):
    hi = a.astype(BF16)
    return hi, (a - hi.astype(F32)).astype(BF16)


def dot(a, b):
    return jnp.dot(a, b, preferred_element_type=F32)


def dot_wide(a, b):
    wide = jnp.concatenate(b, axis=1)
    high, low = dot(a[0], wide), dot(a[1], wide)
    n = b[0].shape[1]
    return high[:, :n] + (high[:, n:] + low[:, :n])


def dot3(a, b):
    return dot(a[0], b[0]) + (dot(a[0], b[1]) + dot(a[1], b[0]))


FIELD_ROWS = 128
POT_ROWS = 16
MESSAGE = FIELD_ROWS + POT_ROWS


def spread_kernel(v_hbm, pot_hbm, out_hbm, v_ref, pot_ref, out_ref, in_sems, out_sems):
    pot_load = pltpu.make_async_copy(pot_hbm, pot_ref, in_sems.at[SLAB])
    pot_load.start()
    loads = [
        pltpu.make_async_copy(v_hbm.at[x], v_ref.at[x], in_sems.at[x]) for x in range(SLAB)
    ]
    for load in loads:
        load.start()

    def store(t):
        rows = pl.ds(32 * t, 32 if t < 4 else POT_ROWS)
        return pltpu.make_async_copy(
            out_ref.at[:, :, rows], out_hbm.at[:, :, rows], out_sems.at[t]
        )

    pot_load.wait()
    pot = jnp.concatenate([pot_ref[:, y, :] for y in range(NY)], axis=1)
    half = jnp.where(lax.axis_index("c") == 0, pot[:4], pot[4:])
    for k in range(2):
        tile = jnp.concatenate(
            [half[:, 256 * k + 128 * u : 256 * k + 128 * (u + 1)] for u in range(2)], axis=0
        )
        rows = pl.ds(FIELD_ROWS + 8 * k, 8)
        out_ref[:, :, rows, :] = jnp.broadcast_to(tile, (16, 2, 8, 128))
    store(4).start()
    for t in range(4):
        loads[2 * t].wait()
        loads[2 * t + 1].wait()
        a = v_ref[2 * t].T.reshape(16, 8, PLANE)
        b = v_ref[2 * t + 1].T.reshape(16, 8, PLANE)
        low = low_rows(a.shape)
        even = jnp.where(low, a, swap_halves(b))
        odd = jnp.where(low, swap_halves(a), b)
        for k in range(4):
            rows, lanes = pl.ds(32 * t + 8 * k, 8), slice(128 * k, 128 * (k + 1))
            out_ref[:, 0, rows, :] = even[:, :, lanes]
            out_ref[:, 1, rows, :] = odd[:, :, lanes]
        store(t).start()
    for t in range(5):
        store(t).wait()


def spread(field, potential):
    shape = (16, 2, MESSAGE, 128)
    out = pl.pallas_call(
        spread_kernel,
        in_specs=[pl.BlockSpec(memory_space=pl.ANY)] * 2,
        out_specs=pl.BlockSpec(memory_space=pl.ANY),
        out_shape=jax.ShapeDtypeStruct(shape, F32),
        scratch_shapes=[
            pltpu.VMEM((SLAB, PLANE, 128), F32),
            pltpu.VMEM((SLAB, NY, NZ), F32),
            pltpu.VMEM(shape, F32),
            pltpu.SemaphoreType.DMA((SLAB + 1,)),
            pltpu.SemaphoreType.DMA((5,)),
        ],
        compiler_params=pltpu.CompilerParams(vmem_limit_bytes=VMEM_SPREAD),
        name="spread",
    )(field, potential)
    return out.reshape(32 * MESSAGE, 128)


ROWS = 4 * NX
EDGE = 16
CHUNK = 512


CHUNKS = ROWS // CHUNK
PARTS = 32 // CHUNKS


SUB = 128


def beside(wide, count):
    half = pltpu.roll(wide, 4, 0)

    def at(a, shift):
        return a[EDGE + shift : EDGE + shift + count]

    return (
        STENCIL[0] * (at(half, 0) + at(half, 8))
        + STENCIL[1] * (at(wide, 8) + at(wide, -8))
        + (at(half, -8) + at(half, 16))
    )


def neighbours(wide, ring):
    near = dot(jnp.concatenate(split(wide[EDGE : EDGE + CHUNK]), axis=1), ring)
    return near + beside(wide, CHUNK)


def gather_kernel(in_ref, ring_ref, field_ref, sum_ref):
    def planes(s, first, count):
        tiles = in_ref[s, 32 * first : 32 * (first + count), :].reshape(-1, count, 4, 8, 128)
        return jnp.concatenate(
            [tiles[:, :, k].reshape(-1, 128) for k in range(4)], axis=1
        )

    ring = ring_ref[...]
    for i in range(CHUNKS):
        before, after = (PARTS * i - 1) % 32, PARTS * (i + 1) % 32
        middle = planes(slice(PARTS * i, PARTS * (i + 1)), 0, 4)
        wide = jnp.concatenate(
            [
                planes(slice(before, before + 1), 2, 2),
                middle,
                planes(slice(after, after + 1), 0, 2),
            ],
            axis=0,
        )
        rows = pl.ds(CHUNK * i, CHUNK)
        field_ref[rows, :] = middle
        sum_ref[rows, :] = neighbours(wide, ring)


def gather(messages, ring):
    return pl.pallas_call(
        gather_kernel,
        out_shape=(jax.ShapeDtypeStruct((ROWS, PLANE), F32),) * 2,
        compiler_params=pltpu.CompilerParams(vmem_limit_bytes=VMEM),
        name="gather",
    )(messages, ring)


def filter_kernel(
    place_ref, field_ref, sum_ref, mine_ref, other_ref, ring_ref,
    out_ref, one_ref, two_ref, diag_ref, sems,
):
    c = place_ref[1]

    def fill(s, _):
        base = pl.multiple_of(s * 32, 32)
        mine, other = mine_ref[s], other_ref[s]
        low = low_rows((8, 128))
        for h in range(2):
            pot = 0.5 * jnp.where(c == h, mine, other) + 2.0 * DIAGONAL
            for t in range(2):
                tiles = []
                for k in range(4):
                    at = 8 * (k // 2) + 4 * (k % 2) + 2 * t
                    tiles.append(jnp.where(low, pot[at : at + 1], pot[at + 1 : at + 2]))
                diag = jnp.concatenate(tiles, axis=1)
                at = base + 16 * h + 8 * t
                rows = pl.ds(at, 8)
                diag_ref[rows, :] = diag
                one_ref[pl.ds(EDGE + at, 8), :] = (
                    UNIT * sum_ref[rows, :] + 0.5 * diag * field_ref[rows, :]
                )
        return 0

    lax.fori_loop(0, 32, fill, 0, unroll=True)
    ring = ring_ref[...]

    def close(ref):
        ref[0:EDGE, :] = ref[ROWS : ROWS + EDGE, :]
        ref[ROWS + EDGE :, :] = ref[EDGE : 2 * EDGE, :]

    def sweep(cur_ref, emit, finish=None):
        def product(i):
            cur = cur_ref[pl.ds(EDGE + CHUNK * i, CHUNK), :]
            return dot(jnp.concatenate(split(cur), axis=1), ring)

        ahead = product(0)
        for i in range(CHUNKS):
            near, ahead = ahead, product(i + 1) if i + 1 < CHUNKS else None
            for r in range(0, CHUNK, SUB):
                for k in range(0, PLANE, 128):
                    lanes, rows = slice(k, k + 128), pl.ds(CHUNK * i + r, SUB)
                    wide = cur_ref[pl.ds(CHUNK * i + r, SUB + 2 * EDGE), lanes]
                    total = near[r : r + SUB, lanes] + beside(wide, SUB)
                    own = diag_ref[rows, lanes] * wide[EDGE : EDGE + SUB]
                    emit(rows, lanes, (2.0 * UNIT) * total + own)
            if finish is not None:
                finish(CHUNK * i)

    def copy(base):
        return pltpu.make_async_copy(
            two_ref.at[pl.ds(EDGE + base, CHUNK)],
            out_ref.at[pl.ds(base, CHUNK)],
            sems.at[base // CHUNK],
        )

    def padded(rows):
        return pl.ds(EDGE + rows.start, rows.size)

    def second(rows, lanes, value):
        two_ref[padded(rows), lanes] = value - field_ref[rows, lanes]

    def third(rows, lanes, value):
        rows = padded(rows)
        one_ref[rows, lanes] = value - one_ref[rows, lanes]

    def fourth(rows, lanes, value):
        rows = padded(rows)
        two_ref[rows, lanes] = value - two_ref[rows, lanes]

    close(one_ref)
    sweep(one_ref, second)
    close(two_ref)
    sweep(two_ref, third)
    close(one_ref)
    sweep(one_ref, fourth, lambda base: copy(base).start())
    for i in range(CHUNKS):
        copy(CHUNK * i).wait()


def chebyshev(place, field, partial_sum, mine, other, ring):
    smem = pl.BlockSpec(memory_space=pltpu.SMEM)
    vmem = pl.BlockSpec(memory_space=pltpu.VMEM)
    return pl.pallas_call(
        filter_kernel,
        in_specs=[smem] + [vmem] * 5,
        out_shape=jax.ShapeDtypeStruct((ROWS, PLANE), F32),
        scratch_shapes=[
            pltpu.VMEM((ROWS + 2 * EDGE, PLANE), F32),
            pltpu.VMEM((ROWS + 2 * EDGE, PLANE), F32),
            pltpu.VMEM((ROWS, PLANE), F32),
            pltpu.SemaphoreType.DMA((CHUNKS,)),
        ],
        out_specs=pl.BlockSpec(memory_space=pltpu.HBM),
        compiler_params=pltpu.CompilerParams(vmem_limit_bytes=VMEM),
        name="chebyshev",
    )(place, field, partial_sum, mine, other, ring)


BLOCKS = tuple((i, j) for i in range(4) for j in range(i, 4))
PART = 352


def turn_kernel(in_ref, near_ref, far_ref, left_ref, cells_ref):
    for q in range(4):
        a = in_ref[:, 0, q]
        b = in_ref[:, 1, q]
        low = low_rows(a.shape)
        rows = pl.ds(128 * q, 128)
        cells_ref[rows, :PLANE] = jnp.where(low, a, swap_halves(b)).reshape(128, PLANE)
        cells_ref[rows, PLANE:] = jnp.where(low, swap_halves(a), b).reshape(128, PLANE)
    by_orbital = cells_ref[...]
    by_cell = by_orbital.T
    near_ref[...] = by_cell[:PART]
    far_ref[...] = by_cell[PART:]
    left_ref[...] = by_orbital.astype(BF16)


def turn(cells):
    return pl.pallas_call(
        turn_kernel,
        out_shape=(
            jax.ShapeDtypeStruct((PART, NORB), F32),
            jax.ShapeDtypeStruct((2 * PLANE - PART, NORB), F32),
            jax.ShapeDtypeStruct((NORB, 2 * PLANE), BF16),
        ),
        scratch_shapes=[pltpu.VMEM((NORB, 2 * PLANE), F32)],
        compiler_params=pltpu.CompilerParams(vmem_limit_bytes=VMEM_SMALL),
        name="turn",
    )(cells.reshape(16, 2, 4, 8, PLANE))


def gram_kernel(place_ref, near_ref, far_ref, left_ref, mine_ref, other_ref, sums_ref):
    right = split(jnp.concatenate([near_ref[...], far_ref[...]], axis=0))
    square, cross = dot(left_ref[...], right[0]), dot(left_ref[...], right[1])

    def block(a, i, j):
        return a[128 * i : 128 * (i + 1), 128 * j : 128 * (j + 1)]

    for k, (i, j) in enumerate(BLOCKS):
        rows = pl.ds(128 * (k % 5), 128)
        sums_ref[k // 5, rows, :] = block(square, i, j) + (
            block(cross, i, j) + block(cross, j, i).T
        )
    mine_ref[...] = sums_ref[place_ref[1]]
    other_ref[...] = sums_ref[1 - place_ref[1]]


SCALARS = pl.BlockSpec(memory_space=pltpu.SMEM)
VECTORS = pl.BlockSpec(memory_space=pltpu.VMEM)
ANYWHERE = pl.BlockSpec(memory_space=pl.ANY)


def gram(place, near, far, left):
    return pl.pallas_call(
        gram_kernel,
        in_specs=[SCALARS, VECTORS, VECTORS, VECTORS],
        out_shape=(jax.ShapeDtypeStruct((640, 128), F32),) * 2,
        scratch_shapes=[pltpu.VMEM((2, 640, 128), F32)],
        compiler_params=pltpu.CompilerParams(vmem_limit_bytes=VMEM_SMALL),
        name="gram",
    )(place, near, far, left)


def mirrored(a):
    row = lax.broadcasted_iota(jnp.int32, a.shape, 0)
    col = lax.broadcasted_iota(jnp.int32, a.shape, 1)
    return jnp.where(row <= col, a, a.T)


def product(a, b):
    top = dot3([p[:256] for p in a], b)
    low_block = dot_wide([p[256:] for p in a], [p[:, 256:] for p in b])
    return jnp.concatenate(
        [
            jnp.concatenate([mirrored(top[:, :256]), top[:, 256:]], axis=1),
            jnp.concatenate([top[:, 256:].T, mirrored(low_block)], axis=1),
        ],
        axis=0,
    )


def squared(a):
    cross = dot(a[0], a[1])
    return dot(a[0], a[0]) + (cross + cross.T)


def root_kernel(place_ref, mine_ref, other_ref, out_ref):
    zl, c = place_ref[0], place_ref[1]
    blocks = {}
    for k, (i, j) in enumerate(BLOCKS):
        rows = pl.ds(128 * (k % 5), 128)
        mine, other = mine_ref[rows, :], other_ref[rows, :]
        block = jnp.where(c == k // 5, mine, other) * (1.0 / (NX * PLANE))
        blocks[i, j] = block
        if i != j:
            blocks[j, i] = block.T
    total = jnp.concatenate(
        [jnp.concatenate([blocks[i, j] for j in range(4)], axis=1) for i in range(4)], axis=0
    )
    square = jnp.sum(jnp.sum(total * total, axis=0, keepdims=True), axis=1, keepdims=True)
    norm_scale = jnp.sqrt(square + 1e-06)
    row = lax.broadcasted_iota(jnp.int32, (NORB, NORB), 0)
    col = lax.broadcasted_iota(jnp.int32, (NORB, NORB), 1)
    diagonal = row == col
    m = total / norm_scale
    inverse = None
    for pair in range(NS_ITERS // 2):
        parts = split(m)
        m2 = squared(parts)
        base = 0.25 * m2 - 1.125 * m + jnp.where(diagonal, 27.0 / 32.0, 0.0)
        rest = jnp.where(diagonal, 1575.0 / 1024.0, 0.0) - (69.0 / 128.0) * m
        factor = squared(split(base)) + rest
        factors = split(factor)
        if inverse is None:
            chip = jnp.where(zl == 0, factor[:, :256], factor[:, 256:])
            first, second = chip[:, :128], chip[:, 128:]
            inverse = jnp.concatenate(
                [jnp.where(c == 0, first, second), jnp.where(c == 0, second, first)], axis=1
            )
        else:
            inverse = dot_wide(factors, split(inverse))
        if pair < NS_ITERS // 2 - 1:
            m = product(parts, split(squared(factors)))
    root = split(inverse / jnp.sqrt(norm_scale))
    out_ref[0] = root[0]
    out_ref[1] = root[1]


def inverse_root(place, mine, other):
    return pl.pallas_call(
        root_kernel,
        in_specs=[SCALARS, VECTORS, VECTORS],
        out_shape=jax.ShapeDtypeStruct((2, NORB, 256), BF16),
        compiler_params=pltpu.CompilerParams(vmem_limit_bytes=VMEM),
        name="inverse_root",
    )(place, mine, other)


def whiten_kernel(*refs):
    chunks, root_ref, ours_ref, theirs_ref = refs[:-3], refs[-3], refs[-2], refs[-1]
    root = (root_ref[0], root_ref[1])
    start = 0
    for ref in chunks:
        white = dot_wide(split(ref[...]), root)
        rows = pl.ds(start, ref.shape[0])
        ours_ref[rows, :] = white[:, :128]
        theirs_ref[rows, :] = white[:, 128:]
        start += ref.shape[0]


def whiten(chunks, root):
    rows = sum(chunk.shape[0] for chunk in chunks)
    return pl.pallas_call(
        whiten_kernel,
        out_shape=(jax.ShapeDtypeStruct((rows, 128), F32),) * 2,
        compiler_params=pltpu.CompilerParams(vmem_limit_bytes=VMEM_SMALL),
        name="whiten",
    )(*chunks, root)


WHOLE = jax.ShapeDtypeStruct((2, 2, 2 * PLANE, 128), F32)


def place_kernel(jobs, place_ref, *refs):
    whole_ref, sems = refs[-2], refs[-1]
    copies = []
    for k, (part, source, rows, other_chip, other_core, at) in enumerate(jobs):
        zl = 1 - place_ref[0] if other_chip else place_ref[0]
        c = 1 - place_ref[1] if other_core else place_ref[1]
        copies.append(
            pltpu.make_async_copy(
                refs[part].at[pl.ds(source, rows)],
                whole_ref.at[zl, c, pl.ds(at, rows)],
                sems.at[k],
            )
        )
    for copy in copies:
        copy.start()
    for copy in copies:
        copy.wait()


def put(place, jobs, parts, whole=None):
    aliased = () if whole is None else (whole,)
    return pl.pallas_call(
        functools.partial(place_kernel, jobs),
        in_specs=[SCALARS] + [ANYWHERE] * (len(parts) + len(aliased)),
        out_specs=ANYWHERE,
        out_shape=WHOLE,
        scratch_shapes=[pltpu.SemaphoreType.DMA((len(jobs),))],
        input_output_aliases={1 + len(parts): 0} if aliased else {},
        compiler_params=pltpu.CompilerParams(vmem_limit_bytes=VMEM_SMALL),
        name="put",
    )(place, *parts, *aliased)


def exchange(a, axes):
    return lax.all_to_all(a, axes, 0, 0, tiled=True)


def swap(a, axis):
    return lax.ppermute(a, axis, [(0, 1), (1, 0)])


def body(orbitals, potential):
    place = jnp.stack([lax.axis_index("zl"), lax.axis_index("c")])
    ring = jnp.asarray(np.tile(plane_stencil(), (2, 1)), BF16)
    sent = spread(orbitals.reshape(SLAB, PLANE, 128), potential)
    sent, place = lax.optimization_barrier((sent, place))
    messages = exchange(sent, SPACE).reshape(32, MESSAGE, 128)
    half = messages[:, FIELD_ROWS:]
    other_half = swap(half, "c")
    field, partial_sum = gather(messages, ring)
    filtered = chebyshev(place, field, partial_sum, half, other_half, ring)
    near, far, left = turn(exchange(filtered, EVERY))
    mine, other = gram(place, near, far, left)

    other_near = swap(near, "zl")
    share = exchange(mine + swap(other, "c"), ("x", "y"))
    share = jnp.sum(share.reshape(16, -1, 128), axis=0)
    share, other_near = lax.optimization_barrier((share, other_near))
    ring_z = [
        lax.ppermute(share, ("zh", "zl"), [(i, (i + k) % 4) for i in range(4)]) for k in (2, 1, 3)
    ]
    share = (share + ring_z[0]) + (ring_z[1] + ring_z[2])
    share, far = lax.optimization_barrier((share, far))
    other_far = swap(far, "zl")
    total = exchange(jnp.tile(share, (16, 1)), ("x", "y"))
    root = inverse_root(place, total, swap(total, "c"))

    ours, theirs = whiten((near, far, other_near), root)
    first = swap(theirs, "c")
    late_ours, late_theirs = whiten((other_far,), root)
    second = swap(late_theirs, "c")
    chunk, late = 2 * PLANE, 2 * PLANE - PART
    jobs = tuple(
        job
        for part, other_core in ((0, False), (2, True))
        for job in (
            (part, 0, chunk, False, other_core, 0),
            (part, chunk, PART, True, other_core, 0),
        )
    )
    whole = put(place, jobs + ((1, 0, late, True, False, PART),), (ours, late_ours, first))
    whitened = put(place, ((0, 0, late, True, True, PART),), (second,), whole)
    return whitened.reshape(orbitals.shape)


def solution(mesh):
    fine = Mesh(mesh.devices.reshape(4, 2, 4, 2, 2), EVERY)
    return jax.shard_map(
        body,
        mesh=fine,
        in_specs=(P(SPACE, None, None, ORB), P(SPACE, None, None)),
        out_specs=P(SPACE, None, None, ORB),
        check_vma=False,
    )
```

```python
import functools

import numpy as np
import jax
import jax.numpy as jnp
from jax import lax
from jax.experimental import pallas as pl
from jax.experimental.pallas import tpu as pltpu
from jax.sharding import Mesh, PartitionSpec as P

DEGREE = 4
NS_ITERS = 8
NY, NZ = 16, 32
PLANE = NY * NZ
NX = 256
NORB = 512
SLAB = 8
SPACE = ("x", "zh", "y")
ORB = ("zl", "c")
EVERY = SPACE + ORB
F32 = jnp.float32
BF16 = jnp.bfloat16
VMEM = 30 * 1024 * 1024
VMEM_SPREAD = 60 * 1024 * 1024
VMEM_SMALL = 24 * 1024 * 1024

STENCIL = (135.0, -13.5, 1.0)
UNIT = -0.5 / 90.0 / 4.0
DIAGONAL = (1.5 * 49.0 / 18.0 - 5.0) / 4.0


def plane_stencil():
    def ring(n):
        m = np.zeros((n, n), np.float32)
        for k, w in enumerate(STENCIL, 1):
            for i in range(n):
                m[i, (i + k) % n] += w
                m[i, (i - k) % n] += w
        return m

    return np.kron(ring(NY), np.eye(NZ, dtype=np.float32)) + np.kron(
        np.eye(NY, dtype=np.float32), ring(NZ)
    )


def low_rows(shape):
    return lax.broadcasted_iota(jnp.int32, shape, len(shape) - 2) < 4


def swap_halves(a):
    return pltpu.roll(a, 4, a.ndim - 2)


def split(a):
    hi = a.astype(BF16)
    return hi, (a - hi.astype(F32)).astype(BF16)


def dot(a, b):
    return jnp.dot(a, b, preferred_element_type=F32)


def dot_wide(a, b):
    wide = jnp.concatenate(b, axis=1)
    high, low = dot(a[0], wide), dot(a[1], wide)
    n = b[0].shape[1]
    return high[:, :n] + (high[:, n:] + low[:, :n])


def dot3(a, b):
    return dot(a[0], b[0]) + (dot(a[0], b[1]) + dot(a[1], b[0]))


FIELD_ROWS = 128
POT_ROWS = 16
MESSAGE = FIELD_ROWS + POT_ROWS


def spread_kernel(v_hbm, pot_hbm, out_hbm, v_ref, pot_ref, out_ref, in_sems, out_sems):
    pot_load = pltpu.make_async_copy(pot_hbm, pot_ref, in_sems.at[SLAB])
    pot_load.start()
    loads = [
        pltpu.make_async_copy(v_hbm.at[x], v_ref.at[x], in_sems.at[x]) for x in range(SLAB)
    ]
    for load in loads:
        load.start()

    def store(t):
        rows = pl.ds(32 * t, 32 if t < 4 else POT_ROWS)
        return pltpu.make_async_copy(
            out_ref.at[:, :, rows], out_hbm.at[:, :, rows], out_sems.at[t]
        )

    pot_load.wait()
    pot = jnp.concatenate([pot_ref[:, y, :] for y in range(NY)], axis=1)
    half = jnp.where(lax.axis_index("c") == 0, pot[:4], pot[4:])
    for k in range(2):
        tile = jnp.concatenate(
            [half[:, 256 * k + 128 * u : 256 * k + 128 * (u + 1)] for u in range(2)], axis=0
        )
        rows = pl.ds(FIELD_ROWS + 8 * k, 8)
        out_ref[:, :, rows, :] = jnp.broadcast_to(tile, (16, 2, 8, 128))
    store(4).start()
    for t in range(4):
        loads[2 * t].wait()
        loads[2 * t + 1].wait()
        a = v_ref[2 * t].T.reshape(16, 8, PLANE)
        b = v_ref[2 * t + 1].T.reshape(16, 8, PLANE)
        low = low_rows(a.shape)
        even = jnp.where(low, a, swap_halves(b))
        odd = jnp.where(low, swap_halves(a), b)
        for k in range(4):
            rows, lanes = pl.ds(32 * t + 8 * k, 8), slice(128 * k, 128 * (k + 1))
            out_ref[:, 0, rows, :] = even[:, :, lanes]
            out_ref[:, 1, rows, :] = odd[:, :, lanes]
        store(t).start()
    for t in range(5):
        store(t).wait()


def spread(field, potential):
    shape = (16, 2, MESSAGE, 128)
    out = pl.pallas_call(
        spread_kernel,
        in_specs=[pl.BlockSpec(memory_space=pl.ANY)] * 2,
        out_specs=pl.BlockSpec(memory_space=pl.ANY),
        out_shape=jax.ShapeDtypeStruct(shape, F32),
        scratch_shapes=[
            pltpu.VMEM((SLAB, PLANE, 128), F32),
            pltpu.VMEM((SLAB, NY, NZ), F32),
            pltpu.VMEM(shape, F32),
            pltpu.SemaphoreType.DMA((SLAB + 1,)),
            pltpu.SemaphoreType.DMA((5,)),
        ],
        compiler_params=pltpu.CompilerParams(vmem_limit_bytes=VMEM_SPREAD),
        name="spread",
    )(field, potential)
    return out.reshape(32 * MESSAGE, 128)


ROWS = 4 * NX
EDGE = 16
CHUNK = 512


CHUNKS = ROWS // CHUNK
PARTS = 32 // CHUNKS


SUB = 128


def beside(wide, count):
    half = pltpu.roll(wide, 4, 0)

    def at(a, shift):
        return a[EDGE + shift : EDGE + shift + count]

    return (
        STENCIL[0] * (at(half, 0) + at(half, 8))
        + STENCIL[1] * (at(wide, 8) + at(wide, -8))
        + (at(half, -8) + at(half, 16))
    )


def neighbours(wide, ring, count):
    near = dot(jnp.concatenate(split(wide[EDGE : EDGE + count]), axis=1), ring)
    return near + beside(wide, count)


FIRST = 256


def gather_kernel(in_ref, ring_ref, field_ref, sum_ref):
    def planes(s, first, count):
        tiles = in_ref[s, 32 * first : 32 * (first + count), :].reshape(-1, count, 4, 8, 128)
        return jnp.concatenate(
            [tiles[:, :, k].reshape(-1, 128) for k in range(4)], axis=1
        )

    ring = ring_ref[...]
    for i in range((ROWS // FIRST)):
        before, after = ((FIRST // 32) * i - 1) % 32, (FIRST // 32) * (i + 1) % 32
        middle = planes(slice((FIRST // 32) * i, (FIRST // 32) * (i + 1)), 0, 4)
        wide = jnp.concatenate(
            [
                planes(slice(before, before + 1), 2, 2),
                middle,
                planes(slice(after, after + 1), 0, 2),
            ],
            axis=0,
        )
        rows = pl.ds(FIRST * i, FIRST)
        field_ref[rows, :] = middle
        sum_ref[rows, :] = neighbours(wide, ring, FIRST)


def gather(messages, ring):
    return pl.pallas_call(
        gather_kernel,
        out_shape=(jax.ShapeDtypeStruct((ROWS, PLANE), F32),) * 2,
        compiler_params=pltpu.CompilerParams(vmem_limit_bytes=VMEM),
        name="gather",
    )(messages, ring)


def filter_kernel(
    place_ref, field_ref, sum_ref, mine_ref, other_ref, ring_ref,
    out_ref, one_ref, two_ref, diag_ref, sems,
):
    c = place_ref[1]

    def fill(s, _):
        base = pl.multiple_of(s * 32, 32)
        mine, other = mine_ref[s], other_ref[s]
        low = low_rows((8, 128))
        for h in range(2):
            pot = 0.5 * jnp.where(c == h, mine, other) + 2.0 * DIAGONAL
            for t in range(2):
                tiles = []
                for k in range(4):
                    at = 8 * (k // 2) + 4 * (k % 2) + 2 * t
                    tiles.append(jnp.where(low, pot[at : at + 1], pot[at + 1 : at + 2]))
                diag = jnp.concatenate(tiles, axis=1)
                at = base + 16 * h + 8 * t
                rows = pl.ds(at, 8)
                diag_ref[rows, :] = diag
                one_ref[pl.ds(EDGE + at, 8), :] = (
                    UNIT * sum_ref[rows, :] + 0.5 * diag * field_ref[rows, :]
                )
        return 0

    lax.fori_loop(0, 32, fill, 0, unroll=True)
    ring = ring_ref[...]

    def close(ref):
        ref[0:EDGE, :] = ref[ROWS : ROWS + EDGE, :]
        ref[ROWS + EDGE :, :] = ref[EDGE : 2 * EDGE, :]

    def sweep(cur_ref, emit, finish=None):
        def product(i):
            cur = cur_ref[pl.ds(EDGE + CHUNK * i, CHUNK), :]
            return dot(jnp.concatenate(split(cur), axis=1), ring)

        ahead = product(0)
        for i in range(CHUNKS):
            near, ahead = ahead, product(i + 1) if i + 1 < CHUNKS else None
            for r in range(0, CHUNK, SUB):
                for k in range(0, PLANE, 128):
                    lanes, rows = slice(k, k + 128), pl.ds(CHUNK * i + r, SUB)
                    wide = cur_ref[pl.ds(CHUNK * i + r, SUB + 2 * EDGE), lanes]
                    total = near[r : r + SUB, lanes] + beside(wide, SUB)
                    own = diag_ref[rows, lanes] * wide[EDGE : EDGE + SUB]
                    emit(rows, lanes, (2.0 * UNIT) * total + own)
            if finish is not None:
                finish(CHUNK * i)

    def copy(base):
        return pltpu.make_async_copy(
            two_ref.at[pl.ds(EDGE + base, CHUNK)],
            out_ref.at[pl.ds(base, CHUNK)],
            sems.at[base // CHUNK],
        )

    def padded(rows):
        return pl.ds(EDGE + rows.start, rows.size)

    def second(rows, lanes, value):
        two_ref[padded(rows), lanes] = value - field_ref[rows, lanes]

    def third(rows, lanes, value):
        rows = padded(rows)
        one_ref[rows, lanes] = value - one_ref[rows, lanes]

    def fourth(rows, lanes, value):
        rows = padded(rows)
        two_ref[rows, lanes] = value - two_ref[rows, lanes]

    close(one_ref)
    sweep(one_ref, second)
    close(two_ref)
    sweep(two_ref, third)
    close(one_ref)
    sweep(one_ref, fourth, lambda base: copy(base).start())
    for i in range(CHUNKS):
        copy(CHUNK * i).wait()


def chebyshev(place, field, partial_sum, mine, other, ring):
    smem = pl.BlockSpec(memory_space=pltpu.SMEM)
    vmem = pl.BlockSpec(memory_space=pltpu.VMEM)
    return pl.pallas_call(
        filter_kernel,
        in_specs=[smem] + [vmem] * 5,
        out_shape=jax.ShapeDtypeStruct((ROWS, PLANE), F32),
        scratch_shapes=[
            pltpu.VMEM((ROWS + 2 * EDGE, PLANE), F32),
            pltpu.VMEM((ROWS + 2 * EDGE, PLANE), F32),
            pltpu.VMEM((ROWS, PLANE), F32),
            pltpu.SemaphoreType.DMA((CHUNKS,)),
        ],
        out_specs=pl.BlockSpec(memory_space=pltpu.HBM),
        compiler_params=pltpu.CompilerParams(vmem_limit_bytes=VMEM),
        name="chebyshev",
    )(place, field, partial_sum, mine, other, ring)


BLOCKS = tuple((i, j) for i in range(4) for j in range(i, 4))
PART = 352


def turn_kernel(in_ref, near_ref, far_ref, left_ref, cells_ref):
    for q in range(4):
        a = in_ref[:, 0, q]
        b = in_ref[:, 1, q]
        low = low_rows(a.shape)
        rows = pl.ds(128 * q, 128)
        cells_ref[rows, :PLANE] = jnp.where(low, a, swap_halves(b)).reshape(128, PLANE)
        cells_ref[rows, PLANE:] = jnp.where(low, swap_halves(a), b).reshape(128, PLANE)
    by_orbital = cells_ref[...]
    by_cell = by_orbital.T
    near_ref[...] = by_cell[:PART]
    far_ref[...] = by_cell[PART:]
    left_ref[...] = by_orbital.astype(BF16)


def turn(cells):
    return pl.pallas_call(
        turn_kernel,
        out_shape=(
            jax.ShapeDtypeStruct((PART, NORB), F32),
            jax.ShapeDtypeStruct((2 * PLANE - PART, NORB), F32),
            jax.ShapeDtypeStruct((NORB, 2 * PLANE), BF16),
        ),
        scratch_shapes=[pltpu.VMEM((NORB, 2 * PLANE), F32)],
        compiler_params=pltpu.CompilerParams(vmem_limit_bytes=VMEM_SMALL),
        name="turn",
    )(cells.reshape(16, 2, 4, 8, PLANE))


def gram_kernel(place_ref, near_ref, far_ref, left_ref, mine_ref, other_ref, sums_ref):
    right = split(jnp.concatenate([near_ref[...], far_ref[...]], axis=0))
    square, cross = dot(left_ref[...], right[0]), dot(left_ref[...], right[1])

    def block(a, i, j):
        return a[128 * i : 128 * (i + 1), 128 * j : 128 * (j + 1)]

    for k, (i, j) in enumerate(BLOCKS):
        rows = pl.ds(128 * (k % 5), 128)
        sums_ref[k // 5, rows, :] = block(square, i, j) + (
            block(cross, i, j) + block(cross, j, i).T
        )
    mine_ref[...] = sums_ref[place_ref[1]]
    other_ref[...] = sums_ref[1 - place_ref[1]]


SCALARS = pl.BlockSpec(memory_space=pltpu.SMEM)
VECTORS = pl.BlockSpec(memory_space=pltpu.VMEM)
ANYWHERE = pl.BlockSpec(memory_space=pl.ANY)


def gram(place, near, far, left):
    return pl.pallas_call(
        gram_kernel,
        in_specs=[SCALARS, VECTORS, VECTORS, VECTORS],
        out_shape=(jax.ShapeDtypeStruct((640, 128), F32),) * 2,
        scratch_shapes=[pltpu.VMEM((2, 640, 128), F32)],
        compiler_params=pltpu.CompilerParams(vmem_limit_bytes=VMEM_SMALL),
        name="gram",
    )(place, near, far, left)


def mirrored(a):
    row = lax.broadcasted_iota(jnp.int32, a.shape, 0)
    col = lax.broadcasted_iota(jnp.int32, a.shape, 1)
    return jnp.where(row <= col, a, a.T)


def product(a, b):
    top = dot3([p[:256] for p in a], b)
    low_block = dot_wide([p[256:] for p in a], [p[:, 256:] for p in b])
    return jnp.concatenate(
        [
            jnp.concatenate([mirrored(top[:, :256]), top[:, 256:]], axis=1),
            jnp.concatenate([top[:, 256:].T, mirrored(low_block)], axis=1),
        ],
        axis=0,
    )


def squared(a):
    cross = dot(a[0], a[1])
    return dot(a[0], a[0]) + (cross + cross.T)


def root_kernel(place_ref, mine_ref, other_ref, out_ref):
    zl, c = place_ref[0], place_ref[1]
    blocks = {}
    for k, (i, j) in enumerate(BLOCKS):
        rows = pl.ds(128 * (k % 5), 128)
        mine, other = mine_ref[rows, :], other_ref[rows, :]
        block = jnp.where(c == k // 5, mine, other) * (1.0 / (NX * PLANE))
        blocks[i, j] = block
        if i != j:
            blocks[j, i] = block.T
    total = jnp.concatenate(
        [jnp.concatenate([blocks[i, j] for j in range(4)], axis=1) for i in range(4)], axis=0
    )
    square = jnp.sum(jnp.sum(total * total, axis=0, keepdims=True), axis=1, keepdims=True)
    norm_scale = jnp.sqrt(square + 1e-06)
    row = lax.broadcasted_iota(jnp.int32, (NORB, NORB), 0)
    col = lax.broadcasted_iota(jnp.int32, (NORB, NORB), 1)
    diagonal = row == col
    m = total / norm_scale
    inverse = None
    for pair in range(NS_ITERS // 2):
        parts = split(m)
        m2 = squared(parts)
        base = 0.25 * m2 - 1.125 * m + jnp.where(diagonal, 27.0 / 32.0, 0.0)
        rest = jnp.where(diagonal, 1575.0 / 1024.0, 0.0) - (69.0 / 128.0) * m
        factor = squared(split(base)) + rest
        factors = split(factor)
        if inverse is None:
            chip = jnp.where(zl == 0, factor[:, :256], factor[:, 256:])
            first, second = chip[:, :128], chip[:, 128:]
            inverse = jnp.concatenate(
                [jnp.where(c == 0, first, second), jnp.where(c == 0, second, first)], axis=1
            )
        else:
            inverse = dot_wide(factors, split(inverse))
        if pair < NS_ITERS // 2 - 1:
            m = product(parts, split(squared(factors)))
    root = split(inverse / jnp.sqrt(norm_scale))
    out_ref[0] = root[0]
    out_ref[1] = root[1]


def inverse_root(place, mine, other):
    return pl.pallas_call(
        root_kernel,
        in_specs=[SCALARS, VECTORS, VECTORS],
        out_shape=jax.ShapeDtypeStruct((2, NORB, 256), BF16),
        compiler_params=pltpu.CompilerParams(vmem_limit_bytes=VMEM),
        name="inverse_root",
    )(place, mine, other)


def whiten_rows(chunks, root_ref, ours_ref, theirs_ref, finish=None):
    root = (root_ref[0], root_ref[1])
    start = 0
    for ref in chunks:
        white = dot_wide(split(ref[...]), root)
        rows = pl.ds(start, ref.shape[0])
        ours_ref[rows, :] = white[:, :128]
        theirs_ref[rows, :] = white[:, 128:]
        start += ref.shape[0]
        if finish is not None and start == 2 * PLANE:
            finish()


def whiten_kernel(*refs):
    whiten_rows(refs[:-3], *refs[-3:])


def early_kernel(place_ref, near_ref, far_ref, other_ref, root_ref, ours_ref, theirs_ref, whole_ref, sem):
    copy = pltpu.make_async_copy(
        ours_ref.at[pl.ds(0, 2 * PLANE)], whole_ref.at[place_ref[0], place_ref[1]], sem
    )
    whiten_rows((near_ref, far_ref, other_ref), root_ref, ours_ref, theirs_ref, copy.start)
    copy.wait()


def whiten_early(place, chunks, root):
    rows = sum(chunk.shape[0] for chunk in chunks)
    return pl.pallas_call(
        early_kernel,
        in_specs=[SCALARS] + [VECTORS] * 4,
        out_specs=(VECTORS, VECTORS, ANYWHERE),
        out_shape=(jax.ShapeDtypeStruct((rows, 128), F32),) * 2 + (WHOLE,),
        scratch_shapes=[pltpu.SemaphoreType.DMA],
        compiler_params=pltpu.CompilerParams(vmem_limit_bytes=VMEM_SMALL),
        name="whiten_early",
    )(place, *chunks, root)


def whiten(chunks, root):
    rows = sum(chunk.shape[0] for chunk in chunks)
    return pl.pallas_call(
        whiten_kernel,
        out_shape=(jax.ShapeDtypeStruct((rows, 128), F32),) * 2,
        compiler_params=pltpu.CompilerParams(vmem_limit_bytes=VMEM_SMALL),
        name="whiten",
    )(*chunks, root)


WHOLE = jax.ShapeDtypeStruct((2, 2, 2 * PLANE, 128), F32)


def place_kernel(jobs, place_ref, *refs):
    whole_ref, sems = refs[-2], refs[-1]
    copies = []
    for k, (part, source, rows, other_chip, other_core, at) in enumerate(jobs):
        zl = 1 - place_ref[0] if other_chip else place_ref[0]
        c = 1 - place_ref[1] if other_core else place_ref[1]
        copies.append(
            pltpu.make_async_copy(
                refs[part].at[pl.ds(source, rows)],
                whole_ref.at[zl, c, pl.ds(at, rows)],
                sems.at[k],
            )
        )
    for copy in copies:
        copy.start()
    for copy in copies:
        copy.wait()


def put(place, jobs, parts, whole=None):
    aliased = () if whole is None else (whole,)
    return pl.pallas_call(
        functools.partial(place_kernel, jobs),
        in_specs=[SCALARS] + [ANYWHERE] * (len(parts) + len(aliased)),
        out_specs=ANYWHERE,
        out_shape=WHOLE,
        scratch_shapes=[pltpu.SemaphoreType.DMA((len(jobs),))],
        input_output_aliases={1 + len(parts): 0} if aliased else {},
        compiler_params=pltpu.CompilerParams(vmem_limit_bytes=VMEM_SMALL),
        name="put",
    )(place, *parts, *aliased)


def exchange(a, axes):
    return lax.all_to_all(a, axes, 0, 0, tiled=True)


def swap(a, axis):
    return lax.ppermute(a, axis, [(0, 1), (1, 0)])


def body(orbitals, potential):
    place = jnp.stack([lax.axis_index("zl"), lax.axis_index("c")])
    ring = jnp.asarray(np.tile(plane_stencil(), (2, 1)), BF16)
    sent = spread(orbitals.reshape(SLAB, PLANE, 128), potential)
    sent, place = lax.optimization_barrier((sent, place))
    messages = exchange(sent, SPACE).reshape(32, MESSAGE, 128)
    half = messages[:, FIELD_ROWS:]
    other_half = swap(half, "c")
    field, partial_sum = gather(messages, ring)
    filtered = chebyshev(place, field, partial_sum, half, other_half, ring)
    near, far, left = turn(exchange(filtered, EVERY))
    mine, other = gram(place, near, far, left)

    other_near = swap(near, "zl")
    share = exchange(mine + swap(other, "c"), ("x", "y"))
    share = jnp.sum(share.reshape(16, -1, 128), axis=0)
    share, other_near = lax.optimization_barrier((share, other_near))
    ring_z = [
        lax.ppermute(share, ("zh", "zl"), [(i, (i + k) % 4) for i in range(4)]) for k in (2, 1, 3)
    ]
    share = (share + ring_z[0]) + (ring_z[1] + ring_z[2])
    share, far = lax.optimization_barrier((share, far))
    other_far = swap(far, "zl")
    total = exchange(jnp.tile(share, (16, 1)), ("x", "y"))
    root = inverse_root(place, total, swap(total, "c"))

    ours, theirs, whole = whiten_early(place, (near, far, other_near), root)
    first = swap(theirs, "c")
    late_ours, late_theirs = whiten((other_far,), root)
    second = swap(late_theirs, "c")
    chunk, late = 2 * PLANE, 2 * PLANE - PART
    jobs = (
        (0, chunk, PART, True, False, 0),
        (1, 0, late, True, False, PART),
        (2, 0, chunk, False, True, 0),
        (2, chunk, PART, True, True, 0),
    )
    whole = put(place, jobs, (ours, late_ours, first), whole)
    whitened = put(place, ((0, 0, late, True, True, PART),), (second,), whole)
    return whitened.reshape(orbitals.shape)


def solution(mesh):
    fine = Mesh(mesh.devices.reshape(4, 2, 4, 2, 2), EVERY)
    return jax.shard_map(
        body,
        mesh=fine,
        in_specs=(P(SPACE, None, None, ORB), P(SPACE, None, None)),
        out_specs=P(SPACE, None, None, ORB),
        check_vma=False,
    )
```

```python
import functools

import numpy as np
import jax
import jax.numpy as jnp
from jax import lax
from jax.experimental import pallas as pl
from jax.experimental.pallas import tpu as pltpu
from jax.sharding import Mesh, PartitionSpec as P

DEGREE = 4
NS_ITERS = 8
NY, NZ = 16, 32
PLANE = NY * NZ
NX = 256
NORB = 512
SLAB = 8
SPACE = ("x", "zh", "y")
ORB = ("zl", "c")
EVERY = SPACE + ORB
F32 = jnp.float32
BF16 = jnp.bfloat16
VMEM = 30 * 1024 * 1024
VMEM_SPREAD = 60 * 1024 * 1024
VMEM_SMALL = 24 * 1024 * 1024

STENCIL = (135.0, -13.5, 1.0)
UNIT = -0.5 / 90.0 / 4.0
DIAGONAL = (1.5 * 49.0 / 18.0 - 5.0) / 4.0


def plane_stencil():
    def ring(n):
        m = np.zeros((n, n), np.float32)
        for k, w in enumerate(STENCIL, 1):
            for i in range(n):
                m[i, (i + k) % n] += w
                m[i, (i - k) % n] += w
        return m

    return np.kron(ring(NY), np.eye(NZ, dtype=np.float32)) + np.kron(
        np.eye(NY, dtype=np.float32), ring(NZ)
    )


def low_rows(shape):
    return lax.broadcasted_iota(jnp.int32, shape, len(shape) - 2) < 4


def swap_halves(a):
    return pltpu.roll(a, 4, a.ndim - 2)


def split(a):
    hi = a.astype(BF16)
    return hi, (a - hi.astype(F32)).astype(BF16)


def dot(a, b):
    return jnp.dot(a, b, preferred_element_type=F32)


def dot_wide(a, b):
    wide = jnp.concatenate(b, axis=1)
    high, low = dot(a[0], wide), dot(a[1], wide)
    n = b[0].shape[1]
    return high[:, :n] + (high[:, n:] + low[:, :n])


def dot3(a, b):
    return dot(a[0], b[0]) + (dot(a[0], b[1]) + dot(a[1], b[0]))


FIELD_ROWS = 128
POT_ROWS = 16
MESSAGE = FIELD_ROWS + POT_ROWS


def spread_kernel(v_hbm, pot_hbm, out_hbm, v_ref, pot_ref, out_ref, in_sems, out_sems):
    pot_load = pltpu.make_async_copy(pot_hbm, pot_ref, in_sems.at[SLAB])
    pot_load.start()
    loads = [
        pltpu.make_async_copy(v_hbm.at[x], v_ref.at[x], in_sems.at[x]) for x in range(SLAB)
    ]
    for load in loads:
        load.start()

    def store(t, parity):
        rows = pl.ds(32 * t, 32 if t < 4 else POT_ROWS)
        return pltpu.make_async_copy(
            out_ref.at[:, parity, rows], out_hbm.at[:, parity, rows], out_sems.at[t, parity]
        )

    pot_load.wait()
    pot = jnp.concatenate([pot_ref[:, y, :] for y in range(NY)], axis=1)
    half = jnp.where(lax.axis_index("c") == 0, pot[:4], pot[4:])
    for k in range(2):
        tile = jnp.concatenate(
            [half[:, 256 * k + 128 * u : 256 * k + 128 * (u + 1)] for u in range(2)], axis=0
        )
        rows = pl.ds(FIELD_ROWS + 8 * k, 8)
        out_ref[:, :, rows, :] = jnp.broadcast_to(tile, (16, 2, 8, 128))
    for parity in range(2):
        store(4, parity).start()
    for t in range(4):
        loads[2 * t].wait()
        loads[2 * t + 1].wait()
        a = v_ref[2 * t].T.reshape(16, 8, PLANE)
        b = v_ref[2 * t + 1].T.reshape(16, 8, PLANE)
        low = low_rows(a.shape)
        for parity in range(2):
            if parity == 0:
                mixed = jnp.where(low, a, swap_halves(b))
            else:
                mixed = jnp.where(low, swap_halves(a), b)
            for k in range(4):
                rows = pl.ds(32 * t + 8 * k, 8)
                out_ref[:, parity, rows, :] = mixed[:, :, 128 * k : 128 * (k + 1)]
            store(t, parity).start()
    for t in range(5):
        for parity in range(2):
            store(t, parity).wait()


def spread(field, potential):
    shape = (16, 2, MESSAGE, 128)
    out = pl.pallas_call(
        spread_kernel,
        in_specs=[pl.BlockSpec(memory_space=pl.ANY)] * 2,
        out_specs=pl.BlockSpec(memory_space=pl.ANY),
        out_shape=jax.ShapeDtypeStruct(shape, F32),
        scratch_shapes=[
            pltpu.VMEM((SLAB, PLANE, 128), F32),
            pltpu.VMEM((SLAB, NY, NZ), F32),
            pltpu.VMEM(shape, F32),
            pltpu.SemaphoreType.DMA((SLAB + 1,)),
            pltpu.SemaphoreType.DMA((5, 2)),
        ],
        compiler_params=pltpu.CompilerParams(vmem_limit_bytes=VMEM_SPREAD),
        name="spread",
    )(field, potential)
    return out.reshape(32 * MESSAGE, 128)


ROWS = 4 * NX
EDGE = 16
CHUNK = 512


CHUNKS = ROWS // CHUNK
PARTS = 32 // CHUNKS


SUB = 128


def beside(wide, count):
    half = pltpu.roll(wide, 4, 0)

    def at(a, shift):
        return a[EDGE + shift : EDGE + shift + count]

    return (
        STENCIL[0] * (at(half, 0) + at(half, 8))
        + STENCIL[1] * (at(wide, 8) + at(wide, -8))
        + (at(half, -8) + at(half, 16))
    )


def neighbours(wide, ring, count):
    near = dot(jnp.concatenate(split(wide[EDGE : EDGE + count]), axis=1), ring)
    return near + beside(wide, count)


FIRST = 256


def gather_kernel(in_ref, ring_ref, field_ref, sum_ref):
    def planes(s, first, count):
        tiles = in_ref[s, 32 * first : 32 * (first + count), :].reshape(-1, count, 4, 8, 128)
        return jnp.concatenate(
            [tiles[:, :, k].reshape(-1, 128) for k in range(4)], axis=1
        )

    ring = ring_ref[...]
    for i in range(ROWS // FIRST):
        before, after = ((FIRST // 32) * i - 1) % 32, (FIRST // 32) * (i + 1) % 32
        middle = planes(slice((FIRST // 32) * i, (FIRST // 32) * (i + 1)), 0, 4)
        wide = jnp.concatenate(
            [
                planes(slice(before, before + 1), 2, 2),
                middle,
                planes(slice(after, after + 1), 0, 2),
            ],
            axis=0,
        )
        rows = pl.ds(FIRST * i, FIRST)
        field_ref[rows, :] = middle
        sum_ref[rows, :] = neighbours(wide, ring, FIRST)


def gather(messages, ring):
    return pl.pallas_call(
        gather_kernel,
        out_shape=(jax.ShapeDtypeStruct((ROWS, PLANE), F32),) * 2,
        compiler_params=pltpu.CompilerParams(vmem_limit_bytes=VMEM),
        name="gather",
    )(messages, ring)


def filter_kernel(
    place_ref, field_ref, sum_ref, mine_ref, other_ref, ring_ref,
    out_ref, one_ref, two_ref, diag_ref, sems,
):
    c = place_ref[1]

    def fill(s, _):
        base = pl.multiple_of(s * 32, 32)
        mine, other = mine_ref[s], other_ref[s]
        low = low_rows((8, 128))
        for h in range(2):
            pot = 0.5 * jnp.where(c == h, mine, other) + 2.0 * DIAGONAL
            for t in range(2):
                tiles = []
                for k in range(4):
                    at = 8 * (k // 2) + 4 * (k % 2) + 2 * t
                    tiles.append(jnp.where(low, pot[at : at + 1], pot[at + 1 : at + 2]))
                diag = jnp.concatenate(tiles, axis=1)
                at = base + 16 * h + 8 * t
                rows = pl.ds(at, 8)
                diag_ref[rows, :] = diag
                one_ref[pl.ds(EDGE + at, 8), :] = (
                    UNIT * sum_ref[rows, :] + 0.5 * diag * field_ref[rows, :]
                )
        return 0

    lax.fori_loop(0, 32, fill, 0, unroll=True)
    ring = ring_ref[...]

    def close(ref):
        ref[0:EDGE, :] = ref[ROWS : ROWS + EDGE, :]
        ref[ROWS + EDGE :, :] = ref[EDGE : 2 * EDGE, :]

    def sweep(cur_ref, emit, finish=None):
        def product(i):
            cur = cur_ref[pl.ds(EDGE + CHUNK * i, CHUNK), :]
            return dot(jnp.concatenate(split(cur), axis=1), ring)

        ahead = product(0)
        for i in range(CHUNKS):
            near, ahead = ahead, product(i + 1) if i + 1 < CHUNKS else None
            for r in range(0, CHUNK, SUB):
                for k in range(0, PLANE, 128):
                    lanes, rows = slice(k, k + 128), pl.ds(CHUNK * i + r, SUB)
                    wide = cur_ref[pl.ds(CHUNK * i + r, SUB + 2 * EDGE), lanes]
                    total = near[r : r + SUB, lanes] + beside(wide, SUB)
                    own = diag_ref[rows, lanes] * wide[EDGE : EDGE + SUB]
                    emit(rows, lanes, (2.0 * UNIT) * total + own)
            if finish is not None:
                finish(CHUNK * i)

    def copy(base):
        return pltpu.make_async_copy(
            two_ref.at[pl.ds(EDGE + base, CHUNK)],
            out_ref.at[pl.ds(base, CHUNK)],
            sems.at[base // CHUNK],
        )

    def padded(rows):
        return pl.ds(EDGE + rows.start, rows.size)

    def second(rows, lanes, value):
        two_ref[padded(rows), lanes] = value - field_ref[rows, lanes]

    def third(rows, lanes, value):
        rows = padded(rows)
        one_ref[rows, lanes] = value - one_ref[rows, lanes]

    def fourth(rows, lanes, value):
        rows = padded(rows)
        two_ref[rows, lanes] = value - two_ref[rows, lanes]

    close(one_ref)
    sweep(one_ref, second)
    close(two_ref)
    sweep(two_ref, third)
    close(one_ref)
    sweep(one_ref, fourth, lambda base: copy(base).start())
    for i in range(CHUNKS):
        copy(CHUNK * i).wait()


def chebyshev(place, field, partial_sum, mine, other, ring):
    smem = pl.BlockSpec(memory_space=pltpu.SMEM)
    vmem = pl.BlockSpec(memory_space=pltpu.VMEM)
    return pl.pallas_call(
        filter_kernel,
        in_specs=[smem] + [vmem] * 5,
        out_shape=jax.ShapeDtypeStruct((ROWS, PLANE), F32),
        scratch_shapes=[
            pltpu.VMEM((ROWS + 2 * EDGE, PLANE), F32),
            pltpu.VMEM((ROWS + 2 * EDGE, PLANE), F32),
            pltpu.VMEM((ROWS, PLANE), F32),
            pltpu.SemaphoreType.DMA((CHUNKS,)),
        ],
        out_specs=pl.BlockSpec(memory_space=pltpu.HBM),
        compiler_params=pltpu.CompilerParams(vmem_limit_bytes=VMEM),
        name="chebyshev",
    )(place, field, partial_sum, mine, other, ring)


BLOCKS = tuple((i, j) for i in range(4) for j in range(i, 4))
PART = 352


def turn_kernel(in_ref, near_ref, far_ref, left_ref, cells_ref):
    for q in range(4):
        a = in_ref[:, 0, q]
        b = in_ref[:, 1, q]
        low = low_rows(a.shape)
        rows = pl.ds(128 * q, 128)
        cells_ref[rows, :PLANE] = jnp.where(low, a, swap_halves(b)).reshape(128, PLANE)
        cells_ref[rows, PLANE:] = jnp.where(low, swap_halves(a), b).reshape(128, PLANE)
    by_orbital = cells_ref[...]
    by_cell = by_orbital.T
    near_ref[...] = by_cell[:PART]
    far_ref[...] = by_cell[PART:]
    left_ref[...] = by_orbital.astype(BF16)


def turn(cells):
    return pl.pallas_call(
        turn_kernel,
        out_shape=(
            jax.ShapeDtypeStruct((PART, NORB), F32),
            jax.ShapeDtypeStruct((2 * PLANE - PART, NORB), F32),
            jax.ShapeDtypeStruct((NORB, 2 * PLANE), BF16),
        ),
        scratch_shapes=[pltpu.VMEM((NORB, 2 * PLANE), F32)],
        compiler_params=pltpu.CompilerParams(vmem_limit_bytes=VMEM_SMALL),
        name="turn",
    )(cells.reshape(16, 2, 4, 8, PLANE))


def gram_kernel(place_ref, near_ref, far_ref, left_ref, mine_ref, other_ref, sums_ref):
    right = split(jnp.concatenate([near_ref[...], far_ref[...]], axis=0))
    square, cross = dot(left_ref[...], right[0]), dot(left_ref[...], right[1])

    def block(a, i, j):
        return a[128 * i : 128 * (i + 1), 128 * j : 128 * (j + 1)]

    for k, (i, j) in enumerate(BLOCKS):
        rows = pl.ds(128 * (k % 5), 128)
        sums_ref[k // 5, rows, :] = block(square, i, j) + (
            block(cross, i, j) + block(cross, j, i).T
        )
    mine_ref[...] = sums_ref[place_ref[1]]
    other_ref[...] = sums_ref[1 - place_ref[1]]


SCALARS = pl.BlockSpec(memory_space=pltpu.SMEM)
VECTORS = pl.BlockSpec(memory_space=pltpu.VMEM)
ANYWHERE = pl.BlockSpec(memory_space=pl.ANY)


def gram(place, near, far, left):
    return pl.pallas_call(
        gram_kernel,
        in_specs=[SCALARS, VECTORS, VECTORS, VECTORS],
        out_shape=(jax.ShapeDtypeStruct((640, 128), F32),) * 2,
        scratch_shapes=[pltpu.VMEM((2, 640, 128), F32)],
        compiler_params=pltpu.CompilerParams(vmem_limit_bytes=VMEM_SMALL),
        name="gram",
    )(place, near, far, left)


def mirrored(a):
    row = lax.broadcasted_iota(jnp.int32, a.shape, 0)
    col = lax.broadcasted_iota(jnp.int32, a.shape, 1)
    return jnp.where(row <= col, a, a.T)


def product(a, b):
    top = dot3([p[:256] for p in a], b)
    low_block = dot_wide([p[256:] for p in a], [p[:, 256:] for p in b])
    return jnp.concatenate(
        [
            jnp.concatenate([mirrored(top[:, :256]), top[:, 256:]], axis=1),
            jnp.concatenate([top[:, 256:].T, mirrored(low_block)], axis=1),
        ],
        axis=0,
    )


def squared(a):
    cross = dot(a[0], a[1])
    return dot(a[0], a[0]) + (cross + cross.T)


def root_kernel(place_ref, mine_ref, other_ref, out_ref):
    zl, c = place_ref[0], place_ref[1]
    blocks = {}
    for k, (i, j) in enumerate(BLOCKS):
        rows = pl.ds(128 * (k % 5), 128)
        mine, other = mine_ref[rows, :], other_ref[rows, :]
        block = jnp.where(c == k // 5, mine, other) * (1.0 / (NX * PLANE))
        blocks[i, j] = block
        if i != j:
            blocks[j, i] = block.T
    total = jnp.concatenate(
        [jnp.concatenate([blocks[i, j] for j in range(4)], axis=1) for i in range(4)], axis=0
    )
    square = jnp.sum(jnp.sum(total * total, axis=0, keepdims=True), axis=1, keepdims=True)
    norm_scale = jnp.sqrt(square + 1e-06)
    row = lax.broadcasted_iota(jnp.int32, (NORB, NORB), 0)
    col = lax.broadcasted_iota(jnp.int32, (NORB, NORB), 1)
    diagonal = row == col
    m = total / norm_scale
    inverse = None
    for pair in range(NS_ITERS // 2):
        parts = split(m)
        m2 = squared(parts)
        base = 0.25 * m2 - 1.125 * m + jnp.where(diagonal, 27.0 / 32.0, 0.0)
        rest = jnp.where(diagonal, 1575.0 / 1024.0, 0.0) - (69.0 / 128.0) * m
        factor = squared(split(base)) + rest
        factors = split(factor)
        if inverse is None:
            chip = jnp.where(zl == 0, factor[:, :256], factor[:, 256:])
            first, second = chip[:, :128], chip[:, 128:]
            inverse = jnp.concatenate(
                [jnp.where(c == 0, first, second), jnp.where(c == 0, second, first)], axis=1
            )
        else:
            inverse = dot_wide(factors, split(inverse))
        if pair < NS_ITERS // 2 - 1:
            m = product(parts, split(squared(factors)))
    root = split(inverse / jnp.sqrt(norm_scale))
    out_ref[0] = root[0]
    out_ref[1] = root[1]


def inverse_root(place, mine, other):
    return pl.pallas_call(
        root_kernel,
        in_specs=[SCALARS, VECTORS, VECTORS],
        out_shape=jax.ShapeDtypeStruct((2, NORB, 256), BF16),
        compiler_params=pltpu.CompilerParams(vmem_limit_bytes=VMEM),
        name="inverse_root",
    )(place, mine, other)


def whiten_kernel(*refs):
    chunks, root_ref, ours_ref, theirs_ref = refs[:-3], refs[-3], refs[-2], refs[-1]
    root = (root_ref[0], root_ref[1])
    start = 0
    for ref in chunks:
        white = dot_wide(split(ref[...]), root)
        rows = pl.ds(start, ref.shape[0])
        ours_ref[rows, :] = white[:, :128]
        theirs_ref[rows, :] = white[:, 128:]
        start += ref.shape[0]


def whiten(chunks, root):
    rows = sum(chunk.shape[0] for chunk in chunks)
    return pl.pallas_call(
        whiten_kernel,
        out_shape=(jax.ShapeDtypeStruct((rows, 128), F32),) * 2,
        compiler_params=pltpu.CompilerParams(vmem_limit_bytes=VMEM_SMALL),
        name="whiten",
    )(*chunks, root)


WHOLE = jax.ShapeDtypeStruct((2, 2, 2 * PLANE, 128), F32)


def place_kernel(jobs, place_ref, *refs):
    whole_ref, sems = refs[-2], refs[-1]
    copies = []
    for k, (part, source, rows, other_chip, other_core, at) in enumerate(jobs):
        zl = 1 - place_ref[0] if other_chip else place_ref[0]
        c = 1 - place_ref[1] if other_core else place_ref[1]
        copies.append(
            pltpu.make_async_copy(
                refs[part].at[pl.ds(source, rows)],
                whole_ref.at[zl, c, pl.ds(at, rows)],
                sems.at[k],
            )
        )
    for copy in copies:
        copy.start()
    for copy in copies:
        copy.wait()


def put(place, jobs, parts, whole=None):
    aliased = () if whole is None else (whole,)
    return pl.pallas_call(
        functools.partial(place_kernel, jobs),
        in_specs=[SCALARS] + [ANYWHERE] * (len(parts) + len(aliased)),
        out_specs=ANYWHERE,
        out_shape=WHOLE,
        scratch_shapes=[pltpu.SemaphoreType.DMA((len(jobs),))],
        input_output_aliases={1 + len(parts): 0} if aliased else {},
        compiler_params=pltpu.CompilerParams(vmem_limit_bytes=VMEM_SMALL),
        name="put",
    )(place, *parts, *aliased)


def exchange(a, axes):
    return lax.all_to_all(a, axes, 0, 0, tiled=True)


def swap(a, axis):
    return lax.ppermute(a, axis, [(0, 1), (1, 0)])


def body(orbitals, potential):
    place = jnp.stack([lax.axis_index("zl"), lax.axis_index("c")])
    ring = jnp.asarray(np.tile(plane_stencil(), (2, 1)), BF16)
    sent = spread(orbitals.reshape(SLAB, PLANE, 128), potential)
    sent, place = lax.optimization_barrier((sent, place))
    messages = exchange(sent, SPACE).reshape(32, MESSAGE, 128)
    half = messages[:, FIELD_ROWS:]
    other_half = swap(half, "c")
    field, partial_sum = gather(messages, ring)
    filtered = chebyshev(place, field, partial_sum, half, other_half, ring)
    near, far, left = turn(exchange(filtered, EVERY))
    mine, other = gram(place, near, far, left)

    other_near = swap(near, "zl")
    share = exchange(mine + swap(other, "c"), ("x", "y"))
    share = jnp.sum(share.reshape(16, -1, 128), axis=0)
    share, other_near = lax.optimization_barrier((share, other_near))
    ring_z = [
        lax.ppermute(share, ("zh", "zl"), [(i, (i + k) % 4) for i in range(4)]) for k in (2, 1, 3)
    ]
    share = (share + ring_z[0]) + (ring_z[1] + ring_z[2])
    share, far = lax.optimization_barrier((share, far))
    other_far = swap(far, "zl")
    total = exchange(jnp.tile(share, (16, 1)), ("x", "y"))
    root = inverse_root(place, total, swap(total, "c"))

    ours, theirs = whiten((near, far, other_near), root)
    first = swap(theirs, "c")
    late_ours, late_theirs = whiten((other_far,), root)
    second = swap(late_theirs, "c")
    chunk, late = 2 * PLANE, 2 * PLANE - PART
    jobs = tuple(
        job
        for part, other_core in ((0, False), (2, True))
        for job in (
            (part, 0, chunk, False, other_core, 0),
            (part, chunk, PART, True, other_core, 0),
        )
    )
    whole = put(place, jobs + ((1, 0, late, True, False, PART),), (ours, late_ours, first))
    whitened = put(place, ((0, 0, late, True, True, PART),), (second,), whole)
    return whitened.reshape(orbitals.shape)


def solution(mesh):
    fine = Mesh(mesh.devices.reshape(4, 2, 4, 2, 2), EVERY)
    return jax.shard_map(
        body,
        mesh=fine,
        in_specs=(P(SPACE, None, None, ORB), P(SPACE, None, None)),
        out_specs=P(SPACE, None, None, ORB),
        check_vma=False,
    )
```

```python
import functools

import numpy as np
import jax
import jax.numpy as jnp
from jax import lax
from jax.experimental import pallas as pl
from jax.experimental.pallas import tpu as pltpu
from jax.sharding import Mesh, PartitionSpec as P

DEGREE = 4
NS_ITERS = 8
NY, NZ = 16, 32
PLANE = NY * NZ
NX = 256
NORB = 512
SLAB = 8
SPACE = ("x", "zh", "y")
ORB = ("zl", "c")
EVERY = SPACE + ORB
F32 = jnp.float32
BF16 = jnp.bfloat16
VMEM = 30 * 1024 * 1024
VMEM_SPREAD = 60 * 1024 * 1024
VMEM_SMALL = 24 * 1024 * 1024

STENCIL = (135.0, -13.5, 1.0)
UNIT = -0.5 / 90.0 / 4.0
DIAGONAL = (1.5 * 49.0 / 18.0 - 5.0) / 4.0


def plane_stencil():
    def ring(n):
        m = np.zeros((n, n), np.float32)
        for k, w in enumerate(STENCIL, 1):
            for i in range(n):
                m[i, (i + k) % n] += w
                m[i, (i - k) % n] += w
        return m

    return np.kron(ring(NY), np.eye(NZ, dtype=np.float32)) + np.kron(
        np.eye(NY, dtype=np.float32), ring(NZ)
    )


def low_rows(shape):
    return lax.broadcasted_iota(jnp.int32, shape, len(shape) - 2) < 4


def swap_halves(a):
    return pltpu.roll(a, 4, a.ndim - 2)


def split(a):
    hi = a.astype(BF16)
    return hi, (a - hi.astype(F32)).astype(BF16)


def dot(a, b):
    return jnp.dot(a, b, preferred_element_type=F32)


def dot_wide(a, b):
    wide = jnp.concatenate(b, axis=1)
    high, low = dot(a[0], wide), dot(a[1], wide)
    n = b[0].shape[1]
    return high[:, :n] + (high[:, n:] + low[:, :n])


def dot3(a, b):
    return dot(a[0], b[0]) + (dot(a[0], b[1]) + dot(a[1], b[0]))


FIELD_ROWS = 128
POT_ROWS = 16
MESSAGE = FIELD_ROWS + POT_ROWS


def spread_kernel(v_hbm, pot_hbm, out_hbm, v_ref, pot_ref, out_ref, in_sems, out_sems):
    pot_load = pltpu.make_async_copy(pot_hbm, pot_ref, in_sems.at[SLAB])
    pot_load.start()
    loads = [
        pltpu.make_async_copy(v_hbm.at[x], v_ref.at[x], in_sems.at[x]) for x in range(SLAB)
    ]
    for load in loads:
        load.start()

    def store(t):
        rows = pl.ds(32 * t, 32 if t < 4 else POT_ROWS)
        return pltpu.make_async_copy(
            out_ref.at[:, :, rows], out_hbm.at[:, :, rows], out_sems.at[t]
        )

    pot_load.wait()
    pot = jnp.concatenate([pot_ref[:, y, :] for y in range(NY)], axis=1)
    half = jnp.where(lax.axis_index("c") == 0, pot[:4], pot[4:])
    for k in range(2):
        tile = jnp.concatenate(
            [half[:, 256 * k + 128 * u : 256 * k + 128 * (u + 1)] for u in range(2)], axis=0
        )
        rows = pl.ds(FIELD_ROWS + 8 * k, 8)
        out_ref[:, :, rows, :] = jnp.broadcast_to(tile, (16, 2, 8, 128))
    store(4).start()
    for t in range(4):
        loads[2 * t].wait()
        loads[2 * t + 1].wait()
        a = v_ref[2 * t].T.reshape(16, 8, PLANE)
        b = v_ref[2 * t + 1].T.reshape(16, 8, PLANE)
        low = low_rows(a.shape)
        even = jnp.where(low, a, swap_halves(b))
        odd = jnp.where(low, swap_halves(a), b)
        for k in range(4):
            rows, lanes = pl.ds(32 * t + 8 * k, 8), slice(128 * k, 128 * (k + 1))
            out_ref[:, 0, rows, :] = even[:, :, lanes]
            out_ref[:, 1, rows, :] = odd[:, :, lanes]
        store(t).start()
    for t in range(5):
        store(t).wait()


def spread(field, potential):
    shape = (16, 2, MESSAGE, 128)
    out = pl.pallas_call(
        spread_kernel,
        in_specs=[pl.BlockSpec(memory_space=pl.ANY)] * 2,
        out_specs=pl.BlockSpec(memory_space=pl.ANY),
        out_shape=jax.ShapeDtypeStruct(shape, F32),
        scratch_shapes=[
            pltpu.VMEM((SLAB, PLANE, 128), F32),
            pltpu.VMEM((SLAB, NY, NZ), F32),
            pltpu.VMEM(shape, F32),
            pltpu.SemaphoreType.DMA((SLAB + 1,)),
            pltpu.SemaphoreType.DMA((5,)),
        ],
        compiler_params=pltpu.CompilerParams(vmem_limit_bytes=VMEM_SPREAD),
        name="spread",
    )(field, potential)
    return out.reshape(32 * MESSAGE, 128)


ROWS = 4 * NX
EDGE = 16
CHUNK = 512


CHUNKS = ROWS // CHUNK
PARTS = 32 // CHUNKS


SUB = 128


def beside(wide, count):
    half = pltpu.roll(wide, 4, 0)

    def at(a, shift):
        return a[EDGE + shift : EDGE + shift + count]

    return (
        STENCIL[0] * (at(half, 0) + at(half, 8))
        + STENCIL[1] * (at(wide, 8) + at(wide, -8))
        + (at(half, -8) + at(half, 16))
    )


def neighbours(wide, ring, count):
    near = dot(jnp.concatenate(split(wide[EDGE : EDGE + count]), axis=1), ring)
    return near + beside(wide, count)


FIRST = 256


def gather_kernel(in_ref, ring_ref, field_ref, sum_ref):
    def planes(s, first, count):
        tiles = in_ref[s, 32 * first : 32 * (first + count), :].reshape(-1, count, 4, 8, 128)
        return jnp.concatenate(
            [tiles[:, :, k].reshape(-1, 128) for k in range(4)], axis=1
        )

    ring = ring_ref[...]
    for i in range(ROWS // FIRST):
        before, after = ((FIRST // 32) * i - 1) % 32, (FIRST // 32) * (i + 1) % 32
        middle = planes(slice((FIRST // 32) * i, (FIRST // 32) * (i + 1)), 0, 4)
        wide = jnp.concatenate(
            [
                planes(slice(before, before + 1), 2, 2),
                middle,
                planes(slice(after, after + 1), 0, 2),
            ],
            axis=0,
        )
        rows = pl.ds(FIRST * i, FIRST)
        field_ref[rows, :] = middle
        sum_ref[rows, :] = neighbours(wide, ring, FIRST)


def gather(messages, ring):
    return pl.pallas_call(
        gather_kernel,
        out_shape=(jax.ShapeDtypeStruct((ROWS, PLANE), F32),) * 2,
        compiler_params=pltpu.CompilerParams(vmem_limit_bytes=VMEM),
        name="gather",
    )(messages, ring)


def filter_kernel(
    place_ref, field_ref, sum_ref, mine_ref, other_ref, ring_ref,
    out_ref, one_ref, two_ref, diag_ref, sems,
):
    c = place_ref[1]

    def fill(s, _):
        base = pl.multiple_of(s * 32, 32)
        mine, other = mine_ref[s], other_ref[s]
        low = low_rows((8, 128))
        for h in range(2):
            pot = 0.5 * jnp.where(c == h, mine, other) + 2.0 * DIAGONAL
            for t in range(2):
                tiles = []
                for k in range(4):
                    at = 8 * (k // 2) + 4 * (k % 2) + 2 * t
                    tiles.append(jnp.where(low, pot[at : at + 1], pot[at + 1 : at + 2]))
                diag = jnp.concatenate(tiles, axis=1)
                at = base + 16 * h + 8 * t
                rows = pl.ds(at, 8)
                diag_ref[rows, :] = diag
                one_ref[pl.ds(EDGE + at, 8), :] = (
                    UNIT * sum_ref[rows, :] + 0.5 * diag * field_ref[rows, :]
                )
        return 0

    lax.fori_loop(0, 32, fill, 0, unroll=True)
    ring = ring_ref[...]

    def close(ref):
        ref[0:EDGE, :] = ref[ROWS : ROWS + EDGE, :]
        ref[ROWS + EDGE :, :] = ref[EDGE : 2 * EDGE, :]

    def sweep(cur_ref, emit, finish=None):
        def product(i):
            cur = cur_ref[pl.ds(EDGE + CHUNK * i, CHUNK), :]
            return dot(jnp.concatenate(split(cur), axis=1), ring)

        ahead = product(0)
        for i in range(CHUNKS):
            near, ahead = ahead, product(i + 1) if i + 1 < CHUNKS else None
            for r in range(0, CHUNK, SUB):
                for k in range(0, PLANE, 128):
                    lanes, rows = slice(k, k + 128), pl.ds(CHUNK * i + r, SUB)
                    wide = cur_ref[pl.ds(CHUNK * i + r, SUB + 2 * EDGE), lanes]
                    total = near[r : r + SUB, lanes] + beside(wide, SUB)
                    own = diag_ref[rows, lanes] * wide[EDGE : EDGE + SUB]
                    emit(rows, lanes, (2.0 * UNIT) * total + own)
            if finish is not None:
                finish(CHUNK * i)

    def copy(base):
        return pltpu.make_async_copy(
            two_ref.at[pl.ds(EDGE + base, CHUNK)],
            out_ref.at[pl.ds(base, CHUNK)],
            sems.at[base // CHUNK],
        )

    def padded(rows):
        return pl.ds(EDGE + rows.start, rows.size)

    def second(rows, lanes, value):
        two_ref[padded(rows), lanes] = value - field_ref[rows, lanes]

    def third(rows, lanes, value):
        rows = padded(rows)
        one_ref[rows, lanes] = value - one_ref[rows, lanes]

    def fourth(rows, lanes, value):
        rows = padded(rows)
        two_ref[rows, lanes] = value - two_ref[rows, lanes]

    close(one_ref)
    sweep(one_ref, second)
    close(two_ref)
    sweep(two_ref, third)
    close(one_ref)
    sweep(one_ref, fourth, lambda base: copy(base).start())
    for i in range(CHUNKS):
        copy(CHUNK * i).wait()


def chebyshev(place, field, partial_sum, mine, other, ring):
    smem = pl.BlockSpec(memory_space=pltpu.SMEM)
    vmem = pl.BlockSpec(memory_space=pltpu.VMEM)
    return pl.pallas_call(
        filter_kernel,
        in_specs=[smem] + [vmem] * 5,
        out_shape=jax.ShapeDtypeStruct((ROWS, PLANE), F32),
        scratch_shapes=[
            pltpu.VMEM((ROWS + 2 * EDGE, PLANE), F32),
            pltpu.VMEM((ROWS + 2 * EDGE, PLANE), F32),
            pltpu.VMEM((ROWS, PLANE), F32),
            pltpu.SemaphoreType.DMA((CHUNKS,)),
        ],
        out_specs=pl.BlockSpec(memory_space=pltpu.HBM),
        compiler_params=pltpu.CompilerParams(vmem_limit_bytes=VMEM),
        name="chebyshev",
    )(place, field, partial_sum, mine, other, ring)


BLOCKS = tuple((i, j) for i in range(4) for j in range(i, 4))
PART = 352


def turn_kernel(in_ref, near_ref, far_ref, left_ref, cells_ref):
    for q in range(4):
        a = in_ref[:, 0, q]
        b = in_ref[:, 1, q]
        low = low_rows(a.shape)
        rows = pl.ds(128 * q, 128)
        cells_ref[rows, :PLANE] = jnp.where(low, a, swap_halves(b)).reshape(128, PLANE)
        cells_ref[rows, PLANE:] = jnp.where(low, swap_halves(a), b).reshape(128, PLANE)
    by_orbital = cells_ref[...]
    by_cell = by_orbital.T
    near_ref[...] = by_cell[:PART]
    far_ref[...] = by_cell[PART:]
    left_ref[...] = by_orbital.astype(BF16)


def turn(cells):
    return pl.pallas_call(
        turn_kernel,
        out_shape=(
            jax.ShapeDtypeStruct((PART, NORB), F32),
            jax.ShapeDtypeStruct((2 * PLANE - PART, NORB), F32),
            jax.ShapeDtypeStruct((NORB, 2 * PLANE), BF16),
        ),
        scratch_shapes=[pltpu.VMEM((NORB, 2 * PLANE), F32)],
        compiler_params=pltpu.CompilerParams(vmem_limit_bytes=VMEM_SMALL),
        name="turn",
    )(cells.reshape(16, 2, 4, 8, PLANE))


def gram_kernel(place_ref, near_ref, far_ref, left_ref, mine_ref, other_ref, sums_ref):
    right = split(jnp.concatenate([near_ref[...], far_ref[...]], axis=0))
    square, cross = dot(left_ref[...], right[0]), dot(left_ref[...], right[1])

    def block(a, i, j):
        return a[128 * i : 128 * (i + 1), 128 * j : 128 * (j + 1)]

    for k, (i, j) in enumerate(BLOCKS):
        rows = pl.ds(128 * (k % 5), 128)
        sums_ref[k // 5, rows, :] = block(square, i, j) + (
            block(cross, i, j) + block(cross, j, i).T
        )
    mine_ref[...] = sums_ref[place_ref[1]]
    other_ref[...] = sums_ref[1 - place_ref[1]]


SCALARS = pl.BlockSpec(memory_space=pltpu.SMEM)
VECTORS = pl.BlockSpec(memory_space=pltpu.VMEM)
ANYWHERE = pl.BlockSpec(memory_space=pl.ANY)


def gram(place, near, far, left):
    return pl.pallas_call(
        gram_kernel,
        in_specs=[SCALARS, VECTORS, VECTORS, VECTORS],
        out_shape=(jax.ShapeDtypeStruct((640, 128), F32),) * 2,
        scratch_shapes=[pltpu.VMEM((2, 640, 128), F32)],
        compiler_params=pltpu.CompilerParams(vmem_limit_bytes=VMEM_SMALL),
        name="gram",
    )(place, near, far, left)


def mirrored(a):
    row = lax.broadcasted_iota(jnp.int32, a.shape, 0)
    col = lax.broadcasted_iota(jnp.int32, a.shape, 1)
    return jnp.where(row <= col, a, a.T)


def product(a, b):
    top = dot3([p[:256] for p in a], b)
    low_block = dot_wide([p[256:] for p in a], [p[:, 256:] for p in b])
    return jnp.concatenate(
        [
            jnp.concatenate([mirrored(top[:, :256]), top[:, 256:]], axis=1),
            jnp.concatenate([top[:, 256:].T, mirrored(low_block)], axis=1),
        ],
        axis=0,
    )


def squared(a):
    cross = dot(a[0], a[1])
    return dot(a[0], a[0]) + (cross + cross.T)


def root_kernel(place_ref, mine_ref, other_ref, out_ref):
    zl, c = place_ref[0], place_ref[1]
    blocks = {}
    for k, (i, j) in enumerate(BLOCKS):
        rows = pl.ds(128 * (k % 5), 128)
        mine, other = mine_ref[rows, :], other_ref[rows, :]
        block = jnp.where(c == k // 5, mine, other) * (1.0 / (NX * PLANE))
        blocks[i, j] = block
        if i != j:
            blocks[j, i] = block.T
    total = jnp.concatenate(
        [jnp.concatenate([blocks[i, j] for j in range(4)], axis=1) for i in range(4)], axis=0
    )
    square = jnp.sum(jnp.sum(total * total, axis=0, keepdims=True), axis=1, keepdims=True)
    norm_scale = jnp.sqrt(square + 1e-06)
    row = lax.broadcasted_iota(jnp.int32, (NORB, NORB), 0)
    col = lax.broadcasted_iota(jnp.int32, (NORB, NORB), 1)
    diagonal = row == col
    m = total / norm_scale
    inverse = None
    for pair in range(NS_ITERS // 2):
        parts = split(m)
        m2 = squared(parts)
        base = 0.25 * m2 - 1.125 * m + jnp.where(diagonal, 27.0 / 32.0, 0.0)
        rest = jnp.where(diagonal, 1575.0 / 1024.0, 0.0) - (69.0 / 128.0) * m
        factor = squared(split(base)) + rest
        factors = split(factor)
        if inverse is None:
            chip = jnp.where(zl == 0, factor[:, :256], factor[:, 256:])
            first, second = chip[:, :128], chip[:, 128:]
            inverse = jnp.concatenate(
                [jnp.where(c == 0, first, second), jnp.where(c == 0, second, first)], axis=1
            )
        else:
            inverse = dot_wide(factors, split(inverse))
        if pair < NS_ITERS // 2 - 1:
            m = product(parts, split(squared(factors)))
    root = split(inverse / jnp.sqrt(norm_scale))
    out_ref[0] = root[0]
    out_ref[1] = root[1]


def inverse_root(place, mine, other):
    return pl.pallas_call(
        root_kernel,
        in_specs=[SCALARS, VECTORS, VECTORS],
        out_shape=jax.ShapeDtypeStruct((2, NORB, 256), BF16),
        compiler_params=pltpu.CompilerParams(vmem_limit_bytes=VMEM),
        name="inverse_root",
    )(place, mine, other)


def whiten_kernel(*refs):
    chunks, root_ref, ours_ref, theirs_ref = refs[:-3], refs[-3], refs[-2], refs[-1]
    root = (root_ref[0], root_ref[1])
    start = 0
    for ref in chunks:
        white = dot_wide(split(ref[...]), root)
        rows = pl.ds(start, ref.shape[0])
        ours_ref[rows, :] = white[:, :128]
        theirs_ref[rows, :] = white[:, 128:]
        start += ref.shape[0]


def whiten(chunks, root):
    rows = sum(chunk.shape[0] for chunk in chunks)
    return pl.pallas_call(
        whiten_kernel,
        out_shape=(jax.ShapeDtypeStruct((rows, 128), F32),) * 2,
        compiler_params=pltpu.CompilerParams(vmem_limit_bytes=VMEM_SMALL),
        name="whiten",
    )(*chunks, root)


WHOLE = jax.ShapeDtypeStruct((2, 2, 2 * PLANE, 128), F32)


def place_kernel(jobs, place_ref, *refs):
    whole_ref, sems = refs[-2], refs[-1]
    copies = []
    for k, (part, source, rows, other_chip, other_core, at) in enumerate(jobs):
        zl = 1 - place_ref[0] if other_chip else place_ref[0]
        c = 1 - place_ref[1] if other_core else place_ref[1]
        copies.append(
            pltpu.make_async_copy(
                refs[part].at[pl.ds(source, rows)],
                whole_ref.at[zl, c, pl.ds(at, rows)],
                sems.at[k],
            )
        )
    for copy in copies:
        copy.start()
    for copy in copies:
        copy.wait()


def put(place, jobs, parts, whole=None):
    aliased = () if whole is None else (whole,)
    return pl.pallas_call(
        functools.partial(place_kernel, jobs),
        in_specs=[SCALARS] + [ANYWHERE] * (len(parts) + len(aliased)),
        out_specs=ANYWHERE,
        out_shape=WHOLE,
        scratch_shapes=[pltpu.SemaphoreType.DMA((len(jobs),))],
        input_output_aliases={1 + len(parts): 0} if aliased else {},
        compiler_params=pltpu.CompilerParams(vmem_limit_bytes=VMEM_SMALL),
        name="put",
    )(place, *parts, *aliased)


def exchange(a, axes):
    return lax.all_to_all(a, axes, 0, 0, tiled=True)


def swap(a, axis):
    return lax.ppermute(a, axis, [(0, 1), (1, 0)])


def body(orbitals, potential):
    place = jnp.stack([lax.axis_index("zl"), lax.axis_index("c")])
    ring = jnp.asarray(np.tile(plane_stencil(), (2, 1)), BF16)
    sent = spread(orbitals.reshape(SLAB, PLANE, 128), potential)
    sent, place = lax.optimization_barrier((sent, place))
    messages = exchange(sent, SPACE).reshape(32, MESSAGE, 128)
    half = messages[:, FIELD_ROWS:]
    other_half = swap(half, "c")
    field, partial_sum = gather(messages, ring)
    filtered = chebyshev(place, field, partial_sum, half, other_half, ring)
    near, far, left = turn(exchange(filtered, EVERY))
    mine, other = gram(place, near, far, left)

    other_near = swap(near, "zl")
    share = exchange(mine + swap(other, "c"), ("x", "y"))
    share = jnp.sum(share.reshape(16, -1, 128), axis=0)
    share, other_near = lax.optimization_barrier((share, other_near))
    ring_z = [
        lax.ppermute(share, ("zh", "zl"), [(i, (i + k) % 4) for i in range(4)]) for k in (2, 1, 3)
    ]
    share = (share + ring_z[0]) + (ring_z[1] + ring_z[2])
    share, far = lax.optimization_barrier((share, far))
    other_far = swap(far, "zl")
    total = exchange(jnp.tile(share, (16, 1)), ("x", "y"))
    root = inverse_root(place, total, swap(total, "c"))

    ours, theirs = whiten((near, far, other_near), root)
    first = swap(theirs, "c")
    late_ours, late_theirs = whiten((other_far,), root)
    second = swap(late_theirs, "c")
    chunk, late = 2 * PLANE, 2 * PLANE - PART
    jobs = tuple(
        job
        for part, other_core in ((0, False), (2, True))
        for job in (
            (part, 0, chunk, False, other_core, 0),
            (part, chunk, PART, True, other_core, 0),
        )
    )
    whole = put(place, jobs + ((1, 0, late, True, False, PART),), (ours, late_ours, first))
    whitened = put(place, ((0, 0, late, True, True, PART),), (second,), whole)
    return whitened.reshape(orbitals.shape)


def solution(mesh):
    fine = Mesh(mesh.devices.reshape(4, 2, 4, 2, 2), EVERY)
    return jax.shard_map(
        body,
        mesh=fine,
        in_specs=(P(SPACE, None, None, ORB), P(SPACE, None, None)),
        out_specs=P(SPACE, None, None, ORB),
        check_vma=False,
    )
```
